512 devices in a mesh: dp: 32 (over z, core), mp: 16 (over x, y).
Axes of the slice: x: 4, y: 4, z: 16, core: 2. Of those that a mesh axis runs over, the one named last changes fastest.
Arguments:
- acts: bfloat16 [65536, 8192], P('dp', 'mp'), may hold values from -54 to 54, as said below
- grads_out: bfloat16 [65536, 8192], P('dp', 'mp'), may hold values from -54 to 54, as said below
- panel_owner: int32 [32], replicated, may hold values from 0 to 31, each once
Outputs:
- update: float32 [16, 512, 512], P(None, 'dp', 'mp')
The draws below stay inside these ranges and needn't reach their ends.
Inputs may be any that keep to these rules, and one draw needn't show every extreme that they name: acts: every entry finite. grads_out: every entry finite. `panel_owner`: a permutation of the panels.
All inputs are finite; a program needn't handle non-finite values.
Results may differ from the reference program's by a relative error of at most 0.0003.
Values sent between devices are 32-bit elements; how exact they have to be, the bound alone decides.
No kernel may reach another device: no remote copies, remote signals or barrier semaphores. Data moves between devices by JAX's collectives and lax.ppermute only.
A program may use at most 64 MiB of HBM per device.

```python
import math
import jax
import jax.numpy as jnp
from jax import lax

BS = 512
TOK_DEV = 2048
ITERS = 2
TOKENS = 65536
NBLK = 16
PR = 16
N_DP = 32


def column_spread(key, cols):
    return jnp.exp(jax.random.uniform(key, (cols,), jnp.float32, 0.0, math.log(10.0)))


def base_field(key, rows, cols, spread_wide):
    base = jax.random.truncated_normal(key, -spread_wide, spread_wide, (rows, cols), jnp.float32)
    return base


def draw_acts(key, part):
    key = jax.random.fold_in(key, 11)
    base_key, spread_key = jax.random.split(key, 2)
    cols = NBLK * BS
    ramp = 1.0 + 2.0 * (jnp.arange(cols) % BS).astype(jnp.float32) / BS
    spread = column_spread(spread_key, cols) * ramp
    base = base_field(base_key, TOKENS, cols, 6.0)
    return (0.3 * base * spread[None, :]).astype(jnp.bfloat16)


def draw_grads_out(key, part):
    key = jax.random.fold_in(key, 23)
    base_key, spread_key = jax.random.split(key, 2)
    cols = NBLK * BS
    ramp = 1.0 + 2.0 * jnp.arange(TOKENS).astype(jnp.float32) / TOKENS
    spread = column_spread(spread_key, cols)
    base = base_field(base_key, TOKENS, cols, 6.0)
    return (0.3 * base * ramp[:, None] * spread[None, :]).astype(jnp.bfloat16)


def setup_inputs(seed: int = 0) -> dict:
    key_list = jax.random.split(jax.random.key(seed), 4)
    acts = draw_acts(jax.random.fold_in(key_list[3], 71), 0)
    grads_out = draw_grads_out(jax.random.fold_in(key_list[3], 71), 0)
    panel_owner = jax.random.permutation(key_list[2], N_DP).astype(jnp.int32)
    return dict(acts=acts, grads_out=grads_out, panel_owner=panel_owner)


def matmul(left, right):
    return jnp.matmul(left, right, precision=lax.Precision.HIGHEST)

def one_block(acts, grads_out, panel_owner, index):
    start = (index * BS).astype(jnp.int32)
    inputs = lax.dynamic_slice_in_dim(acts, start, BS, 1).astype(jnp.float32)
    outputs = lax.dynamic_slice_in_dim(grads_out, start, BS, 1).astype(jnp.float32)
    inputs = inputs.reshape(N_DP, TOK_DEV, BS)
    outputs = outputs.reshape(N_DP, TOK_DEV, BS)
    part_grad = jnp.einsum('ntb,ntc->nbc', inputs, outputs, precision=lax.Precision.HIGHEST)
    part_low = lax.optimization_barrier(part_grad.astype(jnp.bfloat16)).astype(jnp.float32)
    left_factor = jnp.einsum('nik,njk->ij', part_low, part_low, precision=lax.Precision.HIGHEST)
    right_factor = jnp.einsum('nki,nkj->ij', part_low, part_low, precision=lax.Precision.HIGHEST)
    grad_sum = lax.optimization_barrier(jnp.sum(part_grad, axis=0))
    factors = jnp.stack([left_factor, right_factor])
    norm_f = jnp.sqrt(lax.optimization_barrier(jnp.sum(factors * factors, axis=(1, 2))) + 1e-06)
    identity = jnp.eye(BS, dtype=jnp.float32)[None]
    iterate_m = factors / norm_f[:, None, None]
    iterate_z = (5.0 * identity - iterate_m) / 4.0
    iterate_x = norm_f[:, None, None] ** (-0.25) * iterate_z
    for step in range(1, ITERS):
        square = matmul(iterate_z, iterate_z)
        iterate_m = matmul(iterate_m, matmul(square, square))
        iterate_z = (5.0 * identity - iterate_m) / 4.0
        iterate_x = matmul(iterate_x, iterate_z)
    precond = matmul(matmul(iterate_x[0], grad_sum), iterate_x[1])
    scale_rms = jnp.sqrt(jnp.mean(precond * precond) + 1e-06)
    ordered = precond.reshape(N_DP, PR, BS)[panel_owner].reshape(BS, BS)
    return ordered / scale_rms

def reference(acts, grads_out, panel_owner):
    indices = jnp.arange(NBLK, dtype=jnp.int32)
    return lax.map(lambda index: one_block(acts, grads_out, panel_owner, index), indices)
```

```python
import functools

import jax
import jax.numpy as jnp
import numpy as np
from jax import lax
from jax.experimental import pallas as pl
from jax.experimental.pallas import tpu as pltpu
from jax.sharding import PartitionSpec as P

Z = 16
W = 512
B = 128
GROWS = 128
FROWS = 160
OFF = ((0, 1), (0, 2), (0, 3), (1, 2), (1, 3), (2, 3))
VMEM_LIMIT = 40 * 1024 * 1024


def partner1(v):
    return v ^ 1


def partner2(v):
    return (((v + 1) % Z) ^ 1) - 1 if ((v + 1) % Z) ^ 1 else Z - 1


def partner3(v):
    return v + 3 if v % 4 == 0 else v - 3 if v % 4 == 3 else (v + 3) % Z if v % 4 == 2 else (v - 3) % Z


def partner4(v):
    return (v + 5) % Z if v % 2 else (v - 5) % Z


EIGHTH = {3: 0, 8: 0, 0: 1, 11: 1, 7: 2, 12: 2, 4: 3, 15: 3, 9: 4, 14: 4, 1: 5, 6: 5, 5: 6, 10: 6, 2: 7, 13: 7}


def local_order(v):
    four = lambda u: [EIGHTH[u], EIGHTH[partner3(u)], EIGHTH[partner2(u)], EIGHTH[partner3(partner2(u))]]
    return four(v) + four(partner1(v))


def position(z, core):
    return z if core == 0 else (-z) % Z


def table():
    rows = np.zeros((2 * Z, 16), np.int32)
    for z in range(Z):
        for core in range(2):
            for slot, c in enumerate((core, 1 - core)):
                order = local_order(position(z, c))
                assert sorted(order) == list(range(8))
                for k, e in enumerate(order):
                    rows[2 * z + core, 8 * slot + e] = k
    return rows.reshape(-1)


def ring_pairs(partner):
    pairs = []
    for z in range(Z):
        for core in range(2):
            pairs.append((2 * z + core, 2 * position(partner(position(z, core)), core) + core))
    return pairs


CORE_PAIRS = [(i, i ^ 1) for i in range(2 * Z)]
PAIRS = [ring_pairs(p) for p in (partner1, partner2, partner3, partner4)]


def split(x):
    high = x.astype(jnp.bfloat16)
    low = (x - high.astype(jnp.float32)).astype(jnp.bfloat16)
    return high, low


def dot(a, b, dims=((1,), (0,))):
    return lax.dot_general(a, b, (dims, ((), ())), preferred_element_type=jnp.float32)


def product(a, b):
    (ah, al), (bh, bl) = a, b
    return dot(ah, bh) + (dot(ah, bl) + dot(al, bh))


def rows_of(index, size):
    return pl.ds(pl.multiple_of(index * size, size), size)


def pack_grad(tab, grad, own, send):
    dp = lax.axis_index("dp")

    def put(dst, half, slot):
        for e in range(8):
            r, c = half * 256 + (e // 4) * B, (e % 4) * B
            dst[rows_of(tab[dp * 16 + slot * 8 + e], GROWS), :] = grad[r : r + B, c : c + B]

    @pl.when(dp % 2 == 0)
    def _():
        put(own, 0, 0)
        put(send, 1, 1)

    @pl.when(dp % 2 == 1)
    def _():
        put(own, 1, 0)
        put(send, 0, 1)


def pack_factors(tab, grad, own, send, left, right):
    dp = lax.axis_index("dp")
    low = grad[...].astype(jnp.bfloat16)
    left[...] = dot(low, low, ((1,), (1,)))
    right[...] = dot(low, low, ((0,), (0,)))

    def put(dst, src, slot):
        for e in range(8):
            i, j = OFF[e] if e < 6 else (e - 6, e - 6)
            base = pl.multiple_of(tab[dp * 16 + slot * 8 + e] * FROWS, 32)
            dst[pl.ds(base, B), :] = src[i * B : (i + 1) * B, j * B : (j + 1) * B]
            d = 2 + e // 4
            r = d * B + (e % 4) * 32
            dst[pl.ds(pl.multiple_of(base + B, 32), 32), :] = src[r : r + 32, d * B : (d + 1) * B]

    @pl.when(dp % 2 == 0)
    def _():
        put(own, left, 0)
        put(send, right, 1)

    @pl.when(dp % 2 == 1)
    def _():
        put(own, right, 0)
        put(send, left, 1)


def root(tab, near, far, out, packed, factor):
    dp = lax.axis_index("dp")
    packed[: 4 * FROWS, :] = near[...]
    packed[4 * FROWS :, :] = far[...]
    for e in range(8):
        base = pl.multiple_of(tab[dp * 16 + e] * FROWS, 32)
        block = packed[pl.ds(base, B), :]
        i, j = OFF[e] if e < 6 else (e - 6, e - 6)
        factor[i * B : (i + 1) * B, j * B : (j + 1) * B] = block
        if i != j:
            factor[j * B : (j + 1) * B, i * B : (i + 1) * B] = block.T
        d = 2 + e // 4
        r = d * B + (e % 4) * 32
        factor[r : r + 32, d * B : (d + 1) * B] = packed[pl.ds(pl.multiple_of(base + B, 32), 32), :]
    f = factor[...]
    norm = jnp.sqrt(jnp.sum(f * f, keepdims=True) + 1e-06)
    m1 = f / norm
    s1 = split(m1)
    m2 = product(s1, s1)
    s2 = split(m2)
    m3 = product(s2, s1)
    c = 1.0 / 4096.0
    high = (250.0 * c) * m1 - (25.0 * c) * m2 + c * m3
    low = (-5.0 / 16.0 - 3125.0 * c) * m1 + (3125.0 * c) * m2 - (1250.0 * c) * m3
    diagonal = lax.broadcasted_iota(jnp.int32, (W, W), 0) == lax.broadcasted_iota(jnp.int32, (W, W), 1)
    low = low + jnp.where(diagonal, 25.0 / 16.0, 0.0)
    x = low + product(split(m3), split(high))
    out[...] = x * lax.rsqrt(jnp.sqrt(norm))


def finish(tab, owner, x_own, x_other, g_near, g_far, h_near, h_far, out, grad, precond):
    dp = lax.axis_index("dp")
    core = dp % 2

    def take(near, far, half, slot):
        for e in range(8):
            k = tab[dp * 16 + slot * 8 + e]
            r, c = half * 256 + (e // 4) * B, (e % 4) * B

            @pl.when(k < 4)
            def _():
                grad[r : r + B, c : c + B] = near[rows_of(k, GROWS), :]

            @pl.when(k >= 4)
            def _():
                grad[r : r + B, c : c + B] = far[rows_of(k - 4, GROWS), :]

    @pl.when(core == 0)
    def _():
        take(g_near, g_far, 0, 0)
        take(h_near, h_far, 1, 1)

    @pl.when(core == 1)
    def _():
        take(g_near, g_far, 1, 0)
        take(h_near, h_far, 0, 1)

    left = jnp.where(core == 0, x_own[...], x_other[...])
    right = jnp.where(core == 0, x_other[...], x_own[...])
    mixed = product(split(left), split(grad[...]))
    value = product(split(mixed), split(right))
    precond[...] = value
    scale = jnp.sqrt(jnp.sum(value * value, keepdims=True) / (W * W) + 1e-06)
    out[...] = precond[rows_of(owner[dp], 16), :] / scale


def call(kernel, outs, scratch, *args):
    smem = [isinstance(a, tuple) for a in args]
    return pl.pallas_call(
        kernel,
        out_shape=[jax.ShapeDtypeStruct(s, jnp.float32) for s in outs],
        in_specs=[pl.BlockSpec(memory_space=pltpu.SMEM if s else pltpu.VMEM) for s in smem],
        out_specs=[pl.BlockSpec(memory_space=pltpu.VMEM) for _ in outs],
        scratch_shapes=[pltpu.VMEM(s, jnp.float32) for s in scratch],
        compiler_params=pltpu.CompilerParams(vmem_limit_bytes=VMEM_LIMIT),
    )(*[a[0] if s else a for a, s in zip(args, smem)])


def move(x, step):
    return lax.ppermute(x, "dp", CORE_PAIRS if step == 0 else PAIRS[step - 1])


def halve(own, received):
    half = own.shape[0] // 2
    return own[:half] + received[:half], own[half:] + received[half:]


def total(own, send):
    received = move(send, 0)
    for step in (1, 2, 3):
        keep, give = halve(own, received)
        own, received = keep, move(give, step)
    own = own + received
    own = own + move(own, 4)
    own = jnp.concatenate([own, move(own, 3)])
    own = jnp.concatenate([own, move(own, 2)])
    return own, move(own, 1)


def per_device(acts, grads_out, panel_owner):
    tab = jnp.asarray(table())
    part_grad = jnp.einsum("tb,tc->bc", acts, grads_out, preferred_element_type=jnp.float32)
    g_own, g_send = call(pack_grad, [(8 * GROWS, B)] * 2, [], (tab,), part_grad)
    f_own, f_send = call(pack_factors, [(8 * FROWS, B)] * 2, [(W, W)] * 2, (tab,), part_grad)
    f_near, f_far = total(f_own, f_send)
    g_near, g_far = total(g_own, g_send)
    (x_own,) = call(root, [(W, W)], [(8 * FROWS, B), (W, W)], (tab,), f_near, f_far)
    h_near, h_far = move(g_near, 0), move(g_far, 0)
    x_other = move(x_own, 0)
    (panel,) = call(
        finish, [(16, W)], [(W, W)] * 2, (tab,), (panel_owner,), x_own, x_other, g_near, g_far, h_near, h_far
    )
    return lax.all_to_all(panel[None], "mp", split_axis=2, concat_axis=0, tiled=True)


def solution(mesh):
    return jax.shard_map(
        per_device,
        mesh=mesh,
        in_specs=(P("dp", "mp"), P("dp", "mp"), P()),
        out_specs=P(None, "dp", "mp"),
        check_vma=False,
    )
```

```python
import functools

import jax
import jax.numpy as jnp
from jax import lax
from jax.experimental import pallas as pl
from jax.experimental.pallas import tpu as pltpu
from jax.sharding import PartitionSpec as P

Z = 16
W = 512
B = 128
ROWS = 144
OFF = ((0, 1), (0, 2), (0, 3), (1, 2), (1, 3), (2, 3))
JOIN_FLOPS = 4_000_000_000
ADD_FLOPS = 0
ROOT_FLOPS = 0

MIX_FLOPS = 5_000_000_000
TOKENS = 512
FRONT_LIMIT = 51 * 1024 * 1024
VMEM_LIMIT = 40 * 1024 * 1024


def partner1(v):
    return v ^ 1


def partner2(v):
    return (((v + 1) % Z) ^ 1) - 1 if ((v + 1) % Z) ^ 1 else Z - 1


def partner3(v):
    return v + 3 if v % 4 == 0 else v - 3 if v % 4 == 3 else (v + 3) % Z if v % 4 == 2 else (v - 3) % Z


def partner4(v):
    return (v + 5) % Z if v % 2 else (v - 5) % Z


EIGHTH = {3: 0, 8: 0, 0: 1, 11: 1, 7: 2, 12: 2, 4: 3, 15: 3, 9: 4, 14: 4, 1: 5, 6: 5, 5: 6, 10: 6, 2: 7, 13: 7}


def local_order(v):
    four = lambda u: [EIGHTH[u], EIGHTH[partner3(u)], EIGHTH[partner2(u)], EIGHTH[partner3(partner2(u))]]
    return four(v) + four(partner1(v))


def position(z, core):
    return z if core == 0 else (-z) % Z


def order_code(v):
    order = local_order(v)
    return sum(order.index(e) << (3 * e) for e in range(8))


CODES = [order_code(v) for v in range(Z)]


def places(own):
    dp = lax.axis_index("dp")
    z, core = dp // 2, dp % 2
    v = jnp.where((core == 0) == own, z, (Z - z) % Z)
    code = jnp.int32(CODES[0])
    for u in range(1, Z):
        code = jnp.where(v == u, CODES[u], code)
    return [(code >> (3 * e)) & 7 for e in range(8)]


def ring_pairs(partner):
    pairs = []
    for z in range(Z):
        for core in range(2):
            pairs.append((2 * z + core, 2 * position(partner(position(z, core)), core) + core))
    return pairs


CORE_PAIRS = [(i, i ^ 1) for i in range(2 * Z)]
PAIRS = [ring_pairs(p) for p in (partner1, partner2, partner3, partner4)]


def split(x):
    high = x.astype(jnp.bfloat16)
    low = (x - high.astype(jnp.float32)).astype(jnp.bfloat16)
    return high, low


def dot(a, b, dims=((1,), (0,))):
    return lax.dot_general(a, b, (dims, ((), ())), preferred_element_type=jnp.float32)


def product(a, b):
    (ah, al), (bh, bl) = a, b
    return dot(ah, bh) + (dot(ah, bl) + dot(al, bh))


def rows_of(index, size):
    return pl.ds(pl.multiple_of(index * ROWS, 16), size)


def put_gradient(grad, dst, half, place):
    for e in range(8):
        r, c = half * 256 + (e // 4) * B, (e % 4) * B
        dst[rows_of(place[e], B), :] = grad[r : r + B, c : c + B]
        dst[pl.ds(pl.multiple_of(place[e] * ROWS + B, 16), ROWS - B), :] = jnp.zeros((ROWS - B, B), jnp.float32)


def eighth_parts(e):
    if e < 6:
        return [(OFF[e][0] * B, OFF[e][1] * B, B)]
    return [((2 * e - 12) * B, (2 * e - 12) * B, 64), ((2 * e - 11) * B, (2 * e - 11) * B, 64)]


def left_lanes(rows):
    return lax.broadcasted_iota(jnp.int32, (rows, B), 1) < 64


def put_factor(src, dst, place, corners):
    for pair in range(2):
        lower = [src[d * B + 64 : (d + 1) * B, d * B : (d + 1) * B] for d in (2 * pair, 2 * pair + 1)]
        corners[pair * 64 : (pair + 1) * 64, :] = jnp.where(left_lanes(64), pltpu.roll(lower[0], 64, 1), lower[1])
    for e in range(8):
        base = place[e] * ROWS
        at = 0
        for r, c, n in eighth_parts(e):
            dst[pl.ds(pl.multiple_of(base + at, 16), n), :] = src[r : r + n, c : c + B]
            at += n
        dst[pl.ds(pl.multiple_of(base + at, 16), 16), :] = corners[16 * e : 16 * e + 16, :]


def front(acts, grads_out, f_own, f_send, g_own, g_send, a_vmem, g_vmem, grad, left, right, corners, sems):
    copies = []
    for i in range(acts.shape[0] // TOKENS):
        rows = pl.ds(i * TOKENS, TOKENS)
        pair = [
            pltpu.make_async_copy(src.at[rows], dst.at[rows], sems.at[i, n])
            for n, (src, dst) in enumerate(((acts, a_vmem), (grads_out, g_vmem)))
        ]
        for copy in pair:
            copy.start()
        copies.append(pair)
    place, other = places(True), places(False)
    core = lax.axis_index("dp") % 2
    for i, pair in enumerate(copies):
        for copy in pair:
            copy.wait()
        rows = slice(i * TOKENS, (i + 1) * TOKENS)
        part = dot(a_vmem[rows, :], g_vmem[rows, :], ((0,), (0,)))
        grad[...] = part if i == 0 else grad[...] + part
    low = grad[...].astype(jnp.bfloat16)
    left[...] = dot(low, low, ((1,), (1,)))
    right[...] = dot(low, low, ((0,), (0,)))

    @pl.when(core == 0)
    def _():
        put_factor(left, f_own, place, corners)
        put_factor(right, f_send, other, corners)
        put_gradient(grad, g_own, 0, place)
        put_gradient(grad, g_send, 1, other)

    @pl.when(core == 1)
    def _():
        put_factor(right, f_own, place, corners)
        put_factor(left, f_send, other, corners)
        put_gradient(grad, g_own, 1, place)
        put_gradient(grad, g_send, 0, other)


def root(near, far, after, out, packed, factor, corners):
    place = places(True)
    packed[: 4 * ROWS, :] = near[...]
    packed[4 * ROWS :, :] = far[...]
    for e in range(8):
        base = place[e] * ROWS
        at = 0
        for r, c, n in eighth_parts(e):
            block = packed[pl.ds(pl.multiple_of(base + at, 16), n), :]
            factor[r : r + n, c : c + B] = block
            if r != c:
                factor[c : c + B, r : r + n] = block.T
            at += n
        corners[16 * e : 16 * e + 16, :] = packed[pl.ds(pl.multiple_of(base + at, 16), 16), :]
    for d in range(4):
        upper = factor[d * B : d * B + 64, d * B : (d + 1) * B]
        turned = jnp.concatenate([upper, jnp.zeros_like(upper)]).T
        corner = corners[(d // 2) * 64 : (d // 2 + 1) * 64, :]
        if d % 2 == 0:
            corner = pltpu.roll(corner, 64, 1)
        factor[d * B + 64 : (d + 1) * B, d * B : (d + 1) * B] = jnp.where(left_lanes(64), turned[64:, :], corner)
    f = factor[...]
    norm = jnp.sqrt(jnp.sum(f * f, keepdims=True) + 1e-06)
    m1 = f / norm
    s1 = split(m1)
    m2 = product(s1, s1)
    s2 = split(m2)
    m3 = product(s2, s1)
    c = 1.0 / 4096.0
    high = (250.0 * c) * m1 - (25.0 * c) * m2 + c * m3
    low = (-5.0 / 16.0 - 3125.0 * c) * m1 + (3125.0 * c) * m2 - (1250.0 * c) * m3
    diagonal = lax.broadcasted_iota(jnp.int32, (W, W), 0) == lax.broadcasted_iota(jnp.int32, (W, W), 1)
    low = low + jnp.where(diagonal, 25.0 / 16.0, 0.0)
    x = low + product(split(m3), split(high))
    out[...] = x * lax.rsqrt(jnp.sqrt(norm))


def mix(x, g_near, g_far, h_near, h_far, out, grad):
    core = lax.axis_index("dp") % 2
    place, other = places(True), places(False)

    def take(near, far, half, place):
        for e in range(8):
            k = place[e]
            r, c = half * 256 + (e // 4) * B, (e % 4) * B

            @pl.when(k < 4)
            def _():
                grad[r : r + B, c : c + B] = near[rows_of(k, B), :]

            @pl.when(k >= 4)
            def _():
                grad[r : r + B, c : c + B] = far[rows_of(k - 4, B), :]

    @pl.when(core == 0)
    def _():
        take(g_near, g_far, 0, place)
        take(h_near, h_far, 1, other)
        out[...] = product(split(x[...]), split(grad[...]))

    @pl.when(core == 1)
    def _():
        take(g_near, g_far, 1, place)
        take(h_near, h_far, 0, other)
        out[...] = product(split(grad[...]), split(x[...]))


def finish(owner, mixed, x, out, precond):
    dp = lax.axis_index("dp")

    @pl.when(dp % 2 == 0)
    def _():
        precond[...] = product(split(mixed[...]), split(x[...]))

    @pl.when(dp % 2 == 1)
    def _():
        precond[...] = product(split(x[...]), split(mixed[...]))

    value = precond[...]
    scale = jnp.sqrt(jnp.sum(value * value, keepdims=True) / (W * W) + 1e-06)
    panel = precond[pl.ds(pl.multiple_of(owner[dp] * 16, 16), 16), :] / scale
    lane = lax.broadcasted_iota(jnp.int32, (8, B), 1)
    for m in range(16):
        tile = panel[:, (m // 4) * B : (m // 4 + 1) * B]
        shift = -32 * (m % 4) % B
        upper = pltpu.roll(tile[:8], shift, 1) if shift else tile[:8]
        lower = pltpu.roll(tile[8:], (shift + 32) % B, 1) if (shift + 32) % B else tile[8:]
        out[m] = jnp.where(lane < 32, upper, jnp.where(lane < 64, lower, 0.0))


def unfold(tiles, out):
    out[:, :8, :] = tiles[:, :, :32]
    out[:, 8:, :] = tiles[:, :, 32:64]


def call(kernel, outs, scratch, *args, cost=None):
    places = {tuple: pltpu.SMEM, list: pl.ANY}
    estimate = {} if cost is None else dict(cost_estimate=pl.CostEstimate(flops=cost, transcendentals=0, bytes_accessed=1))
    return pl.pallas_call(
        kernel,
        out_shape=[jax.ShapeDtypeStruct(s, jnp.float32) for s in outs],
        in_specs=[pl.BlockSpec(memory_space=places.get(type(a), pltpu.VMEM)) for a in args],
        out_specs=[pl.BlockSpec(memory_space=pltpu.VMEM) for _ in outs],
        scratch_shapes=[pltpu.VMEM(s, jnp.float32) for s in scratch],
        compiler_params=pltpu.CompilerParams(vmem_limit_bytes=VMEM_LIMIT),
        **estimate,
    )(*[a[0] if type(a) in places else a for a in args])


def move(x, step):
    return lax.ppermute(x, "dp", CORE_PAIRS if step == 0 else PAIRS[step - 1])


def halve(own, received, after):
    half = own.shape[0] // 2

    def kernel(own, received, after, keep, give):
        give[...] = own[half:, :] + received[half:, :]
        keep[...] = own[:half, :] + received[:half, :]

    return call(kernel, [(half, B)] * 2, [], own, received, [after], cost=ADD_FLOPS)


def add(own, received, after):
    def kernel(own, received, after, out):
        out[...] = own[...] + received[...]

    return call(kernel, [own.shape], [], own, received, [after], cost=ADD_FLOPS)[0]


def join(near, far, after):
    half = near.shape[0]

    def kernel(near, far, after, out):
        out[:half, :] = near[...]
        out[half:, :] = far[...]

    return call(kernel, [(2 * half, B)], [], near, far, [after], cost=JOIN_FLOPS)[0]


def totals(first, second):
    (a, a_send), (b, b_send) = first, second
    def move_a(x, step):
        with jax.named_scope("factors"):
            return move(x, step)

    def move_b(x, step):
        with jax.named_scope("grad"):
            return move(x, step)

    a_in, b_in = move_a(a_send, 0), move_b(b_send, 0)
    for step in (1, 2, 3):
        a, a_give = halve(a, a_in, b)
        a_in = move_a(a_give, step)
        b, b_give = halve(b, b_in, a)
        b_in = move_b(b_give, step)
    for step in (4, 3):
        a = add(a, a_in, b)
        a_in = move_a(a, step)
        b = add(b, b_in, a)
        b_in = move_b(b, step)
    for step in (2, 1):
        a = join(a, a_in, b)
        a_in = move_a(a, step)
        b = join(b, b_in, a)
        b_in = move_b(b, step)
    return (a, a_in), (b, b_in)


def per_device(acts, grads_out, panel_owner):
    whole = (8 * ROWS, B)
    f_own, f_send, g_own, g_send = pl.pallas_call(
        front,
        out_shape=[jax.ShapeDtypeStruct(whole, jnp.float32)] * 4,
        in_specs=[pl.BlockSpec(memory_space=pltpu.HBM)] * 2,
        out_specs=[pl.BlockSpec(memory_space=pltpu.VMEM)] * 4,
        scratch_shapes=[pltpu.VMEM(acts.shape, acts.dtype)] * 2
        + [pltpu.VMEM((W, W), jnp.float32)] * 3
        + [pltpu.VMEM((B, B), jnp.float32), pltpu.SemaphoreType.DMA((acts.shape[0] // TOKENS, 2))],
        compiler_params=pltpu.CompilerParams(vmem_limit_bytes=FRONT_LIMIT),
    )(acts, grads_out)
    (f_near, f_far), (g_near, g_far) = totals((f_own, f_send), (g_own, g_send))
    with jax.named_scope("grad"):
        h_near, h_far = move(g_near, 0), move(g_far, 0)
    after = g_near
    (x_own,) = call(root, [(W, W)], [whole, (W, W), (B, B)], f_near, f_far, [after], cost=ROOT_FLOPS)
    with jax.named_scope("root"):
        x_other = move(x_own, 0)
    (mixed,) = call(mix, [(W, W)], [(W, W)], x_own, g_near, g_far, h_near, h_far, cost=MIX_FLOPS)
    (tiles,) = call(finish, [(16, 8, B)], [(W, W)], (panel_owner,), mixed, x_other)
    tiles = lax.all_to_all(tiles, "mp", split_axis=0, concat_axis=0, tiled=True)
    return call(unfold, [(16, 16, 32)], [], tiles)[0]


def solution(mesh):
    return jax.shard_map(
        per_device,
        mesh=mesh,
        in_specs=(P("dp", "mp"), P("dp", "mp"), P()),
        out_specs=P(None, "dp", "mp"),
        check_vma=False,
    )
```

```python
import functools

import jax
import jax.numpy as jnp
from jax import lax
from jax.experimental import pallas as pl
from jax.experimental.pallas import tpu as pltpu
from jax.sharding import PartitionSpec as P

Z = 16
W = 512
B = 128
ROWS = 136
OFF = ((0, 1), (0, 2), (0, 3), (1, 2), (1, 3), (2, 3))
F_FINE = True
G_FINE = True
JOIN_FLOPS = 4_000_000_000
ADD_FLOPS = 0
ROOT_FLOPS = 0

MIX_FLOPS = 5_000_000_000
TOKENS = 512
FRONT_LIMIT = 51 * 1024 * 1024
VMEM_LIMIT = 40 * 1024 * 1024


def partner1(v):
    return v ^ 1


def partner2(v):
    return (((v + 1) % Z) ^ 1) - 1 if ((v + 1) % Z) ^ 1 else Z - 1


def partner3(v):
    return v + 3 if v % 4 == 0 else v - 3 if v % 4 == 3 else (v + 3) % Z if v % 4 == 2 else (v - 3) % Z


def partner4(v):
    return (v + 5) % Z if v % 2 else (v - 5) % Z


EIGHTH = {3: 0, 8: 0, 0: 1, 11: 1, 7: 2, 12: 2, 4: 3, 15: 3, 9: 4, 14: 4, 1: 5, 6: 5, 5: 6, 10: 6, 2: 7, 13: 7}


def holders(v, partners):
    if not partners:
        return [v]
    return holders(v, partners[:-1]) + holders(partners[-1](v), partners[:-1])


def local_order(v, fine):
    order = [EIGHTH[u] for u in holders(v, (partner3, partner2, partner1) if fine else (partner2, partner1))]
    if not fine:
        order = [e for own in order for e in (own & 6, own | 1)]
    assert sorted(order) == list(range(8))
    return order


def position(z, core):
    return z if core == 0 else (-z) % Z


def order_code(v, fine):
    order = local_order(v, fine)
    return sum(order.index(e) << (3 * e) for e in range(8))


def places(own, fine):
    dp = lax.axis_index("dp")
    z, core = dp // 2, dp % 2
    v = jnp.where((core == 0) == own, z, (Z - z) % Z)
    code = jnp.int32(order_code(0, fine))
    for u in range(1, Z):
        code = jnp.where(v == u, order_code(u, fine), code)
    return [(code >> (3 * e)) & 7 for e in range(8)]


def ring_pairs(partner):
    pairs = []
    for z in range(Z):
        for core in range(2):
            pairs.append((2 * z + core, 2 * position(partner(position(z, core)), core) + core))
    return pairs


CORE_PAIRS = [(i, i ^ 1) for i in range(2 * Z)]
PAIRS = [ring_pairs(p) for p in (partner1, partner2, partner3, partner4)]


def split(x):
    high = x.astype(jnp.bfloat16)
    low = (x - high.astype(jnp.float32)).astype(jnp.bfloat16)
    return high, low


def dot(a, b, dims=((1,), (0,))):
    return lax.dot_general(a, b, (dims, ((), ())), preferred_element_type=jnp.float32)


def product(a, b):
    (ah, al), (bh, bl) = a, b
    return dot(ah, bh) + (dot(ah, bl) + dot(al, bh))


def rows_of(index, size):
    return pl.ds(pl.multiple_of(index * ROWS, 8), size)


def put_gradient(grad, dst, half, place):
    for e in range(8):
        r, c = half * 256 + (e // 4) * B, (e % 4) * B
        dst[rows_of(place[e], B), :] = grad[r : r + B, c : c + B]
        dst[pl.ds(pl.multiple_of(place[e] * ROWS + B, 8), ROWS - B), :] = jnp.zeros((ROWS - B, B), jnp.float32)


def block_iota():
    return (lax.broadcasted_iota(jnp.int32, (B, B), n) for n in range(2))


def put_factor(src, dst, place):
    row, col = block_iota()
    for e in range(8):
        base = place[e] * ROWS
        extra = jnp.zeros((ROWS - B, B), jnp.float32)
        if e < 6:
            i, j = OFF[e]
            block = src[i * B : (i + 1) * B, j * B : (j + 1) * B]
        else:
            i = 2 * e - 12
            first = src[i * B : (i + 1) * B, i * B : (i + 1) * B]
            second = src[(i + 1) * B : (i + 2) * B, (i + 1) * B : (i + 2) * B]
            block = jnp.where(row <= col, first, second)
            extra = extra + jnp.sum(jnp.where(row == col, second, 0.0), axis=0, keepdims=True)
        dst[pl.ds(pl.multiple_of(base, 8), B), :] = block
        dst[pl.ds(pl.multiple_of(base + B, 8), ROWS - B), :] = extra


def take_factor(packed, factor, place):
    row, col = block_iota()
    for e in range(8):
        base = place[e] * ROWS
        block = packed[pl.ds(pl.multiple_of(base, 8), B), :]
        turned = block.T
        if e < 6:
            i, j = OFF[e]
            factor[i * B : (i + 1) * B, j * B : (j + 1) * B] = block
            factor[j * B : (j + 1) * B, i * B : (i + 1) * B] = turned
        else:
            i = 2 * e - 12
            diagonal = packed[pl.ds(pl.multiple_of(base + B, 8), ROWS - B), :][:1, :]
            factor[i * B : (i + 1) * B, i * B : (i + 1) * B] = jnp.where(row <= col, block, turned)
            factor[(i + 1) * B : (i + 2) * B, (i + 1) * B : (i + 2) * B] = jnp.where(
                row > col, block, jnp.where(row < col, turned, diagonal)
            )


def front(acts, grads_out, f_own, f_send, g_own, g_send, a_vmem, g_vmem, grad, left, right, sems):
    copies = []
    for i in range(acts.shape[0] // TOKENS):
        rows = pl.ds(i * TOKENS, TOKENS)
        pair = [
            pltpu.make_async_copy(src.at[rows], dst.at[rows], sems.at[i, n])
            for n, (src, dst) in enumerate(((acts, a_vmem), (grads_out, g_vmem)))
        ]
        for copy in pair:
            copy.start()
        copies.append(pair)
    f_place, f_other = places(True, F_FINE), places(False, F_FINE)
    g_place, g_other = places(True, G_FINE), places(False, G_FINE)
    core = lax.axis_index("dp") % 2
    for i, pair in enumerate(copies):
        for copy in pair:
            copy.wait()
        rows = slice(i * TOKENS, (i + 1) * TOKENS)
        part = dot(a_vmem[rows, :], g_vmem[rows, :], ((0,), (0,)))
        grad[...] = part if i == 0 else grad[...] + part
    low = grad[...].astype(jnp.bfloat16)
    left[...] = dot(low, low, ((1,), (1,)))
    right[...] = dot(low, low, ((0,), (0,)))

    @pl.when(core == 0)
    def _():
        put_factor(left, f_own, f_place)
        put_factor(right, f_send, f_other)
        put_gradient(grad, g_own, 0, g_place)
        put_gradient(grad, g_send, 1, g_other)

    @pl.when(core == 1)
    def _():
        put_factor(right, f_own, f_place)
        put_factor(left, f_send, f_other)
        put_gradient(grad, g_own, 1, g_place)
        put_gradient(grad, g_send, 0, g_other)


def root(near, far, after, out, packed, factor):
    packed[: 4 * ROWS, :] = near[...]
    packed[4 * ROWS :, :] = far[...]
    take_factor(packed, factor, places(True, F_FINE))
    f = factor[...]
    norm = jnp.sqrt(jnp.sum(f * f, keepdims=True) + 1e-06)
    m1 = f / norm
    s1 = split(m1)
    m2 = product(s1, s1)
    s2 = split(m2)
    m3 = product(s2, s1)
    c = 1.0 / 4096.0
    high = (250.0 * c) * m1 - (25.0 * c) * m2 + c * m3
    low = (-5.0 / 16.0 - 3125.0 * c) * m1 + (3125.0 * c) * m2 - (1250.0 * c) * m3
    diagonal = lax.broadcasted_iota(jnp.int32, (W, W), 0) == lax.broadcasted_iota(jnp.int32, (W, W), 1)
    low = low + jnp.where(diagonal, 25.0 / 16.0, 0.0)
    x = low + product(split(m3), split(high))
    out[...] = x * lax.rsqrt(jnp.sqrt(norm))


def mix(x, own, other, high, low, grad):
    core = lax.axis_index("dp") % 2

    def take(src, half, place):
        for e in range(8):
            r, c = half * 256 + (e // 4) * B, (e % 4) * B
            grad[r : r + B, c : c + B] = src[rows_of(place[e], B), :]

    def put(value):
        high[...], low[...] = split(value)

    @pl.when(core == 0)
    def _():
        take(own, 0, places(True, G_FINE))
        take(other, 1, places(False, G_FINE))
        put(product(split(x[...]), split(grad[...])))

    @pl.when(core == 1)
    def _():
        take(own, 1, places(True, G_FINE))
        take(other, 0, places(False, G_FINE))
        put(product(split(grad[...]), split(x[...])))


def finish(owner, high, low, x, out, precond):
    dp = lax.axis_index("dp")

    @pl.when(dp % 2 == 0)
    def _():
        precond[...] = product((high[...], low[...]), split(x[...]))

    @pl.when(dp % 2 == 1)
    def _():
        precond[...] = product(split(x[...]), (high[...], low[...]))

    value = precond[...]
    scale = jnp.sqrt(jnp.sum(value * value, keepdims=True) / (W * W) + 1e-06)
    panel = precond[pl.ds(pl.multiple_of(owner[dp] * 16, 16), 16), :] / scale
    lane = lax.broadcasted_iota(jnp.int32, (8, B), 1)
    for m in range(16):
        tile = panel[:, (m // 4) * B : (m // 4 + 1) * B]
        shift = -32 * (m % 4) % B
        upper = pltpu.roll(tile[:8], shift, 1) if shift else tile[:8]
        lower = pltpu.roll(tile[8:], (shift + 32) % B, 1) if (shift + 32) % B else tile[8:]
        out[m] = jnp.where(lane < 32, upper, jnp.where(lane < 64, lower, 0.0))


def unfold(tiles, out):
    out[:, :8, :] = tiles[:, :, :32]
    out[:, 8:, :] = tiles[:, :, 32:64]


def call(kernel, outs, scratch, *args, cost=None, dtype=jnp.float32):
    places = {tuple: pltpu.SMEM, list: pl.ANY}
    estimate = {} if cost is None else dict(cost_estimate=pl.CostEstimate(flops=cost, transcendentals=0, bytes_accessed=1))
    return pl.pallas_call(
        kernel,
        out_shape=[jax.ShapeDtypeStruct(s, dtype) for s in outs],
        in_specs=[pl.BlockSpec(memory_space=places.get(type(a), pltpu.VMEM)) for a in args],
        out_specs=[pl.BlockSpec(memory_space=pltpu.VMEM) for _ in outs],
        scratch_shapes=[pltpu.VMEM(s, jnp.float32) for s in scratch],
        compiler_params=pltpu.CompilerParams(vmem_limit_bytes=VMEM_LIMIT),
        **estimate,
    )(*[a[0] if type(a) in places else a for a in args])


def move(x, step):
    return lax.ppermute(x, "dp", CORE_PAIRS if step == 0 else PAIRS[step - 1])


def halve(own, received, after):
    half = own.shape[0] // 2

    def kernel(own, received, after, keep, give):
        give[...] = own[half:, :] + received[half:, :]
        keep[...] = own[:half, :] + received[:half, :]

    return call(kernel, [(half, B)] * 2, [], own, received, [after], cost=ADD_FLOPS)


def add(own, received, after):
    def kernel(own, received, after, out):
        out[...] = own[...] + received[...]

    return call(kernel, [own.shape], [], own, received, [after], cost=ADD_FLOPS)[0]


def join(near, far, after):
    half = near.shape[0]

    def kernel(near, far, after, out):
        out[:half, :] = near[...]
        out[half:, :] = far[...]

    return call(kernel, [(2 * half, B)], [], near, far, [after], cost=JOIN_FLOPS)[0]


FINE = ((halve, 1), (halve, 2), (halve, 3), (add, 4), (add, 3), (join, 2), (join, 1))
COARSE = ((halve, 1), (halve, 2), (add, 3), (add, 4), (add, 2), (join, 1))
WAYS = {True: FINE, False: COARSE}


def totals(first, second):
    (a, a_send), (b, b_send) = first, second
    def move_a(x, step):
        with jax.named_scope("factors"):
            return move(x, step)

    def move_b(x, step):
        with jax.named_scope("grad"):
            return move(x, step)

    def advance(own, received, after, way, move):
        combine, step = way
        if combine is halve:
            own, give = halve(own, received, after)
            return own, move(give, step)
        own = combine(own, received, after)
        return own, move(own, step)

    a_in, b_in = move_a(a_send, 0), move_b(b_send, 0)
    a_way, b_way = WAYS[F_FINE], WAYS[G_FINE]
    for i in range(max(len(a_way), len(b_way))):
        if i < len(a_way):
            a, a_in = advance(a, a_in, b, a_way[i], move_a)
        if i < len(b_way):
            b, b_in = advance(b, b_in, a, b_way[i], move_b)
    return (a, a_in), (b, b_in)


def per_device(acts, grads_out, panel_owner):
    whole = (8 * ROWS, B)
    f_own, f_send, g_own, g_send = pl.pallas_call(
        front,
        out_shape=[jax.ShapeDtypeStruct(whole, jnp.float32)] * 4,
        in_specs=[pl.BlockSpec(memory_space=pltpu.HBM)] * 2,
        out_specs=[pl.BlockSpec(memory_space=pltpu.VMEM)] * 4,
        scratch_shapes=[pltpu.VMEM(acts.shape, acts.dtype)] * 2
        + [pltpu.VMEM((W, W), jnp.float32)] * 3
        + [pltpu.SemaphoreType.DMA((acts.shape[0] // TOKENS, 2))],
        compiler_params=pltpu.CompilerParams(vmem_limit_bytes=FRONT_LIMIT),
    )(acts, grads_out)
    (f_near, f_far), (g_near, g_far) = totals((f_own, f_send), (g_own, g_send))
    g_sum = join(g_near, g_far, f_near)
    with jax.named_scope("grad"):
        g_other = move(g_sum, 0)
    (x_own,) = call(root, [(W, W)], [whole, (W, W)], f_near, f_far, [g_near], cost=ROOT_FLOPS)
    with jax.named_scope("root"):
        x_other = move(x_own, 0)
    high, low = call(mix, [(W, W)] * 2, [(W, W)], x_own, g_sum, g_other, cost=MIX_FLOPS, dtype=jnp.bfloat16)
    (tiles,) = call(finish, [(16, 8, B)], [(W, W)], (panel_owner,), high, low, x_other)
    tiles = lax.all_to_all(tiles, "mp", split_axis=0, concat_axis=0, tiled=True)
    return call(unfold, [(16, 16, 32)], [], tiles)[0]


def solution(mesh):
    return jax.shard_map(
        per_device,
        mesh=mesh,
        in_specs=(P("dp", "mp"), P("dp", "mp"), P()),
        out_specs=P(None, "dp", "mp"),
        check_vma=False,
    )
```

```python
import functools

import jax
import jax.numpy as jnp
from jax import lax
from jax.experimental import pallas as pl
from jax.experimental.pallas import tpu as pltpu
from jax.sharding import PartitionSpec as P

Z = 16
W = 512
B = 128
ROWS = 136
OFF = ((0, 1), (0, 2), (0, 3), (1, 2), (1, 3), (2, 3))
JOIN_FLOPS = 4_000_000_000
ADD_FLOPS = 0
ROOT_FLOPS = 0

BEGIN_FLOPS = 0
MIX_FLOPS = 5_000_000_000
TOKENS = 512
FRONT_LIMIT = 51 * 1024 * 1024
VMEM_LIMIT = 40 * 1024 * 1024


def partner1(v):
    return v ^ 1


def partner2(v):
    return (((v + 1) % Z) ^ 1) - 1 if ((v + 1) % Z) ^ 1 else Z - 1


def partner3(v):
    return v + 3 if v % 4 == 0 else v - 3 if v % 4 == 3 else (v + 3) % Z if v % 4 == 2 else (v - 3) % Z


def partner4(v):
    return (v + 5) % Z if v % 2 else (v - 5) % Z


EIGHTH = {3: 0, 8: 0, 0: 1, 11: 1, 7: 2, 12: 2, 4: 3, 15: 3, 9: 4, 14: 4, 1: 5, 6: 5, 5: 6, 10: 6, 2: 7, 13: 7}


def holders(v, partners):
    if not partners:
        return [v]
    return holders(v, partners[:-1]) + holders(partners[-1](v), partners[:-1])


def order_code(v):
    order = [EIGHTH[u] for u in holders(v, (partner3, partner2, partner1))]
    assert sorted(order) == list(range(8))
    return sum(order.index(e) << (3 * e) for e in range(8))


def position(z, side):
    return -z % Z if side else z


def role():
    dp = lax.axis_index("dp")
    return (dp // 2 + dp) % 2


def places(own):
    z = lax.axis_index("dp") // 2
    v = jnp.where((role() == 0) == own, z, (Z - z) % Z)
    code = jnp.int32(order_code(0))
    for u in range(1, Z):
        code = jnp.where(v == u, order_code(u), code)
    return [(code >> (3 * e)) & 7 for e in range(8)]


def device(z, side):
    return 2 * z + (z + side) % 2


def ring_pairs(partner):
    pairs = []
    for z in range(Z):
        for side in range(2):
            pairs.append((device(z, side), device(position(partner(position(z, side)), side), side)))
    return pairs


CORE_PAIRS = [(i, i ^ 1) for i in range(2 * Z)]
PAIRS = [CORE_PAIRS] + [ring_pairs(p) for p in (partner1, partner2, partner3, partner4)]


def split(x):
    high = x.astype(jnp.bfloat16)
    low = (x - high.astype(jnp.float32)).astype(jnp.bfloat16)
    return high, low


def dot(a, b, dims=((1,), (0,))):
    return lax.dot_general(a, b, (dims, ((), ())), preferred_element_type=jnp.float32)


def product(a, b):
    (ah, al), (bh, bl) = a, b
    return dot(ah, bh) + (dot(ah, bl) + dot(al, bh))


def rows_of(index, size):
    return pl.ds(pl.multiple_of(index * ROWS, 8), size)


def put_gradient(grad, dst, half, place):
    for e in range(8):
        r, c = half * 256 + (e // 4) * B, (e % 4) * B
        dst[rows_of(place[e], B), :] = grad[r : r + B, c : c + B]
        dst[pl.ds(pl.multiple_of(place[e] * ROWS + B, 8), ROWS - B), :] = jnp.zeros((ROWS - B, B), jnp.float32)


def block_iota():
    return (lax.broadcasted_iota(jnp.int32, (B, B), n) for n in range(2))


def put_factor(src, dst, place):
    row, col = block_iota()
    for e in range(8):
        base = place[e] * ROWS
        extra = jnp.zeros((ROWS - B, B), jnp.float32)
        if e < 6:
            i, j = OFF[e]
            block = src[i * B : (i + 1) * B, j * B : (j + 1) * B]
        else:
            i = 2 * e - 12
            first = src[i * B : (i + 1) * B, i * B : (i + 1) * B]
            second = src[(i + 1) * B : (i + 2) * B, (i + 1) * B : (i + 2) * B]
            block = jnp.where(row <= col, first, second)
            extra = extra + jnp.sum(jnp.where(row == col, second, 0.0), axis=0, keepdims=True)
        dst[pl.ds(pl.multiple_of(base, 8), B), :] = block
        dst[pl.ds(pl.multiple_of(base + B, 8), ROWS - B), :] = extra


def take_factor(packed, factor, place):
    row, col = block_iota()
    for e in range(8):
        base = place[e] * ROWS
        block = packed[pl.ds(pl.multiple_of(base, 8), B), :]
        turned = block.T
        if e < 6:
            i, j = OFF[e]
            factor[i * B : (i + 1) * B, j * B : (j + 1) * B] = block
            factor[j * B : (j + 1) * B, i * B : (i + 1) * B] = turned
        else:
            i = 2 * e - 12
            diagonal = packed[pl.ds(pl.multiple_of(base + B, 8), ROWS - B), :][:1, :]
            factor[i * B : (i + 1) * B, i * B : (i + 1) * B] = jnp.where(row <= col, block, turned)
            factor[(i + 1) * B : (i + 2) * B, (i + 1) * B : (i + 2) * B] = jnp.where(
                row > col, block, jnp.where(row < col, turned, diagonal)
            )


def front(acts, grads_out, f_own, f_send, g_own, g_send, a_vmem, g_vmem, grad, left, right, sems):
    copies = []
    for i in range(acts.shape[0] // TOKENS):
        rows = pl.ds(i * TOKENS, TOKENS)
        pair = [
            pltpu.make_async_copy(src.at[rows], dst.at[rows], sems.at[i, n])
            for n, (src, dst) in enumerate(((acts, a_vmem), (grads_out, g_vmem)))
        ]
        for copy in pair:
            copy.start()
        copies.append(pair)
    place, other = places(True), places(False)
    mine = role()
    for i, pair in enumerate(copies):
        for copy in pair:
            copy.wait()
        rows = slice(i * TOKENS, (i + 1) * TOKENS)
        part = dot(a_vmem[rows, :], g_vmem[rows, :], ((0,), (0,)))
        grad[...] = part if i == 0 else grad[...] + part
    low = grad[...].astype(jnp.bfloat16)
    left[...] = dot(low, low, ((1,), (1,)))
    right[...] = dot(low, low, ((0,), (0,)))

    @pl.when(mine == 0)
    def _():
        put_factor(left, f_own, place)
        put_factor(right, f_send, other)
        put_gradient(grad, g_own, 0, place)
        put_gradient(grad, g_send, 1, other)

    @pl.when(mine == 1)
    def _():
        put_factor(right, f_own, place)
        put_factor(left, f_send, other)
        put_gradient(grad, g_own, 1, place)
        put_gradient(grad, g_send, 0, other)


def root(near, far, after, out, packed, factor):
    packed[: 4 * ROWS, :] = near[...]
    packed[4 * ROWS :, :] = far[...]
    take_factor(packed, factor, places(True))
    f = factor[...]
    norm = jnp.sqrt(jnp.sum(f * f, keepdims=True) + 1e-06)
    m1 = f / norm
    s1 = split(m1)
    m2 = product(s1, s1)
    s2 = split(m2)
    m3 = product(s2, s1)
    c = 1.0 / 4096.0
    high = (250.0 * c) * m1 - (25.0 * c) * m2 + c * m3
    low = (-5.0 / 16.0 - 3125.0 * c) * m1 + (3125.0 * c) * m2 - (1250.0 * c) * m3
    diagonal = lax.broadcasted_iota(jnp.int32, (W, W), 0) == lax.broadcasted_iota(jnp.int32, (W, W), 1)
    low = low + jnp.where(diagonal, 25.0 / 16.0, 0.0)
    x = low + product(split(m3), split(high))
    out[...] = x * lax.rsqrt(jnp.sqrt(norm))


def take_gradient(src, half, place):
    for e in range(8):
        r, c = (e // 4) * B, (e % 4) * B
        half[r : r + B, c : c + B] = src[rows_of(place[e], B), :]
    return split(half[...])


def begin(x, own, out, half):
    mine = role()
    rows = take_gradient(own, half, places(True))

    @pl.when(mine == 0)
    def _():
        out[...] = product(split(x[:, : W // 2]), rows)

    @pl.when(mine == 1)
    def _():
        out[W // 2 :, :] = product(rows, split(x[...]))
        out[: W // 2, :] = jnp.zeros((W // 2, W), jnp.float32)


def mix(x, begun, other, high, low, half):
    mine = role()
    rows = take_gradient(other, half, places(False))

    @pl.when(mine == 0)
    def _():
        high[...], low[...] = split(begun[...] + product(split(x[:, W // 2 :]), rows))

    @pl.when(mine == 1)
    def _():
        high[: W // 2, :], low[: W // 2, :] = split(product(rows, split(x[...])))
        high[W // 2 :, :], low[W // 2 :, :] = split(begun[W // 2 :, :])


def finish(owner, high, low, x, out, precond):
    mine = role()

    @pl.when(mine == 0)
    def _():
        precond[...] = product((high[...], low[...]), split(x[...]))

    @pl.when(mine == 1)
    def _():
        precond[...] = product(split(x[...]), (high[...], low[...]))

    value = precond[...]
    scale = jnp.sqrt(jnp.sum(value * value, keepdims=True) / (W * W) + 1e-06)
    panel = precond[pl.ds(pl.multiple_of(owner[lax.axis_index("dp")] * 16, 16), 16), :] / scale
    lane = lax.broadcasted_iota(jnp.int32, (8, B), 1)
    for m in range(16):
        tile = panel[:, (m // 4) * B : (m // 4 + 1) * B]
        shift = -32 * (m % 4) % B
        upper = pltpu.roll(tile[:8], shift, 1) if shift else tile[:8]
        lower = pltpu.roll(tile[8:], (shift + 32) % B, 1) if (shift + 32) % B else tile[8:]
        out[m] = jnp.where(lane < 32, upper, jnp.where(lane < 64, lower, 0.0))


def unfold(tiles, out):
    out[:, :8, :] = tiles[:, :, :32]
    out[:, 8:, :] = tiles[:, :, 32:64]


def call(kernel, outs, scratch, *args, cost=None, dtype=jnp.float32):
    places = {tuple: pltpu.SMEM, list: pl.ANY}
    estimate = {} if cost is None else dict(cost_estimate=pl.CostEstimate(flops=cost, transcendentals=0, bytes_accessed=1))
    return pl.pallas_call(
        kernel,
        out_shape=[jax.ShapeDtypeStruct(s, dtype) for s in outs],
        in_specs=[pl.BlockSpec(memory_space=places.get(type(a), pltpu.VMEM)) for a in args],
        out_specs=[pl.BlockSpec(memory_space=pltpu.VMEM) for _ in outs],
        scratch_shapes=[pltpu.VMEM(s, jnp.float32) for s in scratch],
        compiler_params=pltpu.CompilerParams(vmem_limit_bytes=VMEM_LIMIT),
        **estimate,
    )(*[a[0] if type(a) in places else a for a in args])


def move(x, step):
    return lax.ppermute(x, "dp", PAIRS[step])


def halve(own, received, after):
    half = own.shape[0] // 2

    def kernel(own, received, after, keep, give):
        give[...] = own[half:, :] + received[half:, :]
        keep[...] = own[:half, :] + received[:half, :]

    return call(kernel, [(half, B)] * 2, [], own, received, [after], cost=ADD_FLOPS)


def add(own, received, after):
    def kernel(own, received, after, out):
        out[...] = own[...] + received[...]

    return call(kernel, [own.shape], [], own, received, [after], cost=ADD_FLOPS)[0]


def join(near, far, after):
    half = near.shape[0]

    def kernel(near, far, after, out):
        out[:half, :] = near[...]
        out[half:, :] = far[...]

    return call(kernel, [(2 * half, B)], [], near, far, [after], cost=JOIN_FLOPS)[0]


WAY = ((halve, 1), (halve, 2), (halve, 3), (add, 4), (add, 3), (join, 2), (join, 1))


def totals(first, second):
    def move_a(x, step):
        with jax.named_scope("factors"):
            return move(x, step)

    def move_b(x, step):
        with jax.named_scope("grad"):
            return move(x, step)

    def advance(own, received, after, combine, step, move):
        if combine is halve:
            own, give = halve(own, received, after)
            return own, move(give, step)
        own = combine(own, received, after)
        return own, move(own, step)

    (a, a_send), (b, b_send) = first, second
    a_in, b_in = move_a(a_send, 0), move_b(b_send, 0)
    for combine, step in WAY:
        a, a_in = advance(a, a_in, b, combine, step, move_a)
        b, b_in = advance(b, b_in, a, combine, step, move_b)
    return (a, a_in), (b, b_in)


def per_device(acts, grads_out, panel_owner):
    whole = (8 * ROWS, B)
    f_own, f_send, g_own, g_send = pl.pallas_call(
        front,
        out_shape=[jax.ShapeDtypeStruct(whole, jnp.float32)] * 4,
        in_specs=[pl.BlockSpec(memory_space=pltpu.HBM)] * 2,
        out_specs=[pl.BlockSpec(memory_space=pltpu.VMEM)] * 4,
        scratch_shapes=[pltpu.VMEM(acts.shape, acts.dtype)] * 2
        + [pltpu.VMEM((W, W), jnp.float32)] * 3
        + [pltpu.SemaphoreType.DMA((acts.shape[0] // TOKENS, 2))],
        compiler_params=pltpu.CompilerParams(vmem_limit_bytes=FRONT_LIMIT),
    )(acts, grads_out)
    (f_near, f_far), (g_near, g_far) = totals((f_own, f_send), (g_own, g_send))
    g_sum = join(g_near, g_far, f_near)
    with jax.named_scope("grad"):
        g_other = move(g_sum, 0)
    (x_own,) = call(root, [(W, W)], [whole, (W, W)], f_near, f_far, [g_near], cost=ROOT_FLOPS)
    with jax.named_scope("root"):
        x_other = move(x_own, 0)
    (begun,) = call(begin, [(W, W)], [(W // 2, W)], x_own, g_sum, cost=BEGIN_FLOPS)
    high, low = call(mix, [(W, W)] * 2, [(W // 2, W)], x_own, begun, g_other, cost=MIX_FLOPS, dtype=jnp.bfloat16)
    (tiles,) = call(finish, [(16, 8, B)], [(W, W)], (panel_owner,), high, low, x_other)
    tiles = lax.all_to_all(tiles, "mp", split_axis=0, concat_axis=0, tiled=True)
    return call(unfold, [(16, 16, 32)], [], tiles)[0]


def solution(mesh):
    return jax.shard_map(
        per_device,
        mesh=mesh,
        in_specs=(P("dp", "mp"), P("dp", "mp"), P()),
        out_specs=P(None, "dp", "mp"),
        check_vma=False,
    )
```

```python
import functools

import jax
import jax.numpy as jnp
from jax import lax
from jax.experimental import pallas as pl
from jax.experimental.pallas import tpu as pltpu
from jax.sharding import PartitionSpec as P

Z = 16
W = 512
B = 128
ROWS = 136
OFF = ((0, 1), (0, 2), (0, 3), (1, 2), (1, 3), (2, 3))
JOIN_FLOPS = 4_000_000_000
ADD_FLOPS = 0
ROOT_FLOPS = 0

BEGIN_FLOPS = 0
MIX_FLOPS = 5_000_000_000
TOKENS = 512
FRONT_LIMIT = 51 * 1024 * 1024
VMEM_LIMIT = 40 * 1024 * 1024


def partner1(v):
    return v ^ 1


def partner2(v):
    return (((v + 1) % Z) ^ 1) - 1 if ((v + 1) % Z) ^ 1 else Z - 1


def partner3(v):
    return v + 3 if v % 4 == 0 else v - 3 if v % 4 == 3 else (v + 3) % Z if v % 4 == 2 else (v - 3) % Z


def partner4(v):
    return (v + 5) % Z if v % 2 else (v - 5) % Z


QUARTER = {0: 0, 3: 0, 8: 0, 11: 0, 4: 1, 7: 1, 12: 1, 15: 1, 1: 2, 6: 2, 9: 2, 14: 2, 2: 3, 5: 3, 10: 3, 13: 3}


def holders(v, partners):
    if not partners:
        return [v]
    return holders(v, partners[:-1]) + holders(partners[-1](v), partners[:-1])


def order_code(v):
    order = [2 * QUARTER[u] + n for u in holders(v, (partner2, partner1)) for n in range(2)]
    assert sorted(order) == list(range(8))
    return sum(order.index(e) << (3 * e) for e in range(8))


def position(z, side):
    return -z % Z if side else z


def role():
    dp = lax.axis_index("dp")
    return (dp // 2 + dp) % 2


def places(own):
    z = lax.axis_index("dp") // 2
    v = jnp.where((role() == 0) == own, z, (Z - z) % Z)
    code = jnp.int32(order_code(0))
    for u in range(1, Z):
        code = jnp.where(v == u, order_code(u), code)
    return [(code >> (3 * e)) & 7 for e in range(8)]


def device(z, side):
    return 2 * z + (z + side) % 2


def ring_pairs(partner):
    pairs = []
    for z in range(Z):
        for side in range(2):
            pairs.append((device(z, side), device(position(partner(position(z, side)), side), side)))
    return pairs


CORE_PAIRS = [(i, i ^ 1) for i in range(2 * Z)]
PAIRS = [CORE_PAIRS] + [ring_pairs(p) for p in (partner1, partner2, partner3, partner4)]


def split(x):
    high = x.astype(jnp.bfloat16)
    low = (x - high.astype(jnp.float32)).astype(jnp.bfloat16)
    return high, low


def dot(a, b, dims=((1,), (0,))):
    return lax.dot_general(a, b, (dims, ((), ())), preferred_element_type=jnp.float32)


def product(a, b):
    (ah, al), (bh, bl) = a, b
    return dot(ah, bh) + (dot(ah, bl) + dot(al, bh))


def rows_of(index, size):
    return pl.ds(pl.multiple_of(index * ROWS, 8), size)


def put_gradient(grad, dst, half, place):
    for e in range(8):
        r, c = half * 256 + (e // 4) * B, (e % 4) * B
        dst[rows_of(place[e], B), :] = grad[r : r + B, c : c + B]
        dst[pl.ds(pl.multiple_of(place[e] * ROWS + B, 8), ROWS - B), :] = jnp.zeros((ROWS - B, B), jnp.float32)


def block_iota():
    return (lax.broadcasted_iota(jnp.int32, (B, B), n) for n in range(2))


def put_factor(src, dst, place):
    row, col = block_iota()
    for e in range(8):
        base = place[e] * ROWS
        extra = jnp.zeros((ROWS - B, B), jnp.float32)
        if e < 6:
            i, j = OFF[e]
            block = src[i * B : (i + 1) * B, j * B : (j + 1) * B]
        else:
            i = 2 * e - 12
            first = src[i * B : (i + 1) * B, i * B : (i + 1) * B]
            second = src[(i + 1) * B : (i + 2) * B, (i + 1) * B : (i + 2) * B]
            block = jnp.where(row <= col, first, second)
            extra = extra + jnp.sum(jnp.where(row == col, second, 0.0), axis=0, keepdims=True)
        dst[pl.ds(pl.multiple_of(base, 8), B), :] = block
        dst[pl.ds(pl.multiple_of(base + B, 8), ROWS - B), :] = extra


def take_factor(packed, factor, place):
    row, col = block_iota()
    for e in range(8):
        base = place[e] * ROWS
        block = packed[pl.ds(pl.multiple_of(base, 8), B), :]
        turned = block.T
        if e < 6:
            i, j = OFF[e]
            factor[i * B : (i + 1) * B, j * B : (j + 1) * B] = block
            factor[j * B : (j + 1) * B, i * B : (i + 1) * B] = turned
        else:
            i = 2 * e - 12
            diagonal = packed[pl.ds(pl.multiple_of(base + B, 8), ROWS - B), :][:1, :]
            factor[i * B : (i + 1) * B, i * B : (i + 1) * B] = jnp.where(row <= col, block, turned)
            factor[(i + 1) * B : (i + 2) * B, (i + 1) * B : (i + 2) * B] = jnp.where(
                row > col, block, jnp.where(row < col, turned, diagonal)
            )


def front(acts, grads_out, f_own, f_send, g_own, g_send, a_vmem, g_vmem, grad, left, right, sems):
    copies = []
    for i in range(acts.shape[0] // TOKENS):
        rows = pl.ds(i * TOKENS, TOKENS)
        pair = [
            pltpu.make_async_copy(src.at[rows], dst.at[rows], sems.at[i, n])
            for n, (src, dst) in enumerate(((acts, a_vmem), (grads_out, g_vmem)))
        ]
        for copy in pair:
            copy.start()
        copies.append(pair)
    place, other = places(True), places(False)
    mine = role()
    for i, pair in enumerate(copies):
        for copy in pair:
            copy.wait()
        rows = slice(i * TOKENS, (i + 1) * TOKENS)
        part = dot(a_vmem[rows, :], g_vmem[rows, :], ((0,), (0,)))
        grad[...] = part if i == 0 else grad[...] + part
    low = grad[...].astype(jnp.bfloat16)
    left[...] = dot(low, low, ((1,), (1,)))
    right[...] = dot(low, low, ((0,), (0,)))

    @pl.when(mine == 0)
    def _():
        put_factor(left, f_own, place)
        put_factor(right, f_send, other)
        put_gradient(grad, g_own, 0, place)
        put_gradient(grad, g_send, 1, other)

    @pl.when(mine == 1)
    def _():
        put_factor(right, f_own, place)
        put_factor(left, f_send, other)
        put_gradient(grad, g_own, 1, place)
        put_gradient(grad, g_send, 0, other)


def root(near, far, after, out, packed, factor):
    packed[: 4 * ROWS, :] = near[...]
    packed[4 * ROWS :, :] = far[...]
    take_factor(packed, factor, places(True))
    f = factor[...]
    norm = jnp.sqrt(jnp.sum(f * f, keepdims=True) + 1e-06)
    m1 = f / norm
    s1 = split(m1)
    m2 = product(s1, s1)
    s2 = split(m2)
    m3 = product(s2, s1)
    c = 1.0 / 4096.0
    high = (250.0 * c) * m1 - (25.0 * c) * m2 + c * m3
    low = (-5.0 / 16.0 - 3125.0 * c) * m1 + (3125.0 * c) * m2 - (1250.0 * c) * m3
    diagonal = lax.broadcasted_iota(jnp.int32, (W, W), 0) == lax.broadcasted_iota(jnp.int32, (W, W), 1)
    low = low + jnp.where(diagonal, 25.0 / 16.0, 0.0)
    x = low + product(split(m3), split(high))
    out[...] = x * lax.rsqrt(jnp.sqrt(norm))


def take_gradient(src, half, place):
    for e in range(8):
        r, c = (e // 4) * B, (e % 4) * B
        half[r : r + B, c : c + B] = src[rows_of(place[e], B), :]
    return split(half[...])


def begin(x, own, out, half):
    mine = role()
    rows = take_gradient(own, half, places(True))

    @pl.when(mine == 0)
    def _():
        out[...] = product(split(x[:, : W // 2]), rows)

    @pl.when(mine == 1)
    def _():
        out[W // 2 :, :] = product(rows, split(x[...]))
        out[: W // 2, :] = jnp.zeros((W // 2, W), jnp.float32)


def mix(x, begun, other, high, low, half):
    mine = role()
    rows = take_gradient(other, half, places(False))

    @pl.when(mine == 0)
    def _():
        high[...], low[...] = split(begun[...] + product(split(x[:, W // 2 :]), rows))

    @pl.when(mine == 1)
    def _():
        high[: W // 2, :], low[: W // 2, :] = split(product(rows, split(x[...])))
        high[W // 2 :, :], low[W // 2 :, :] = split(begun[W // 2 :, :])


def finish(owner, high, low, x, out, precond):
    mine = role()

    @pl.when(mine == 0)
    def _():
        precond[...] = product((high[...], low[...]), split(x[...]))

    @pl.when(mine == 1)
    def _():
        precond[...] = product(split(x[...]), (high[...], low[...]))

    value = precond[...]
    scale = jnp.sqrt(jnp.sum(value * value, keepdims=True) / (W * W) + 1e-06)
    panel = precond[pl.ds(pl.multiple_of(owner[lax.axis_index("dp")] * 16, 16), 16), :] / scale
    lane = lax.broadcasted_iota(jnp.int32, (8, B), 1)
    for m in range(16):
        tile = panel[:, (m // 4) * B : (m // 4 + 1) * B]
        shift = -32 * (m % 4) % B
        upper = pltpu.roll(tile[:8], shift, 1) if shift else tile[:8]
        lower = pltpu.roll(tile[8:], (shift + 32) % B, 1) if (shift + 32) % B else tile[8:]
        out[m] = jnp.where(lane < 32, upper, jnp.where(lane < 64, lower, 0.0))


def unfold(tiles, out):
    out[:, :8, :] = tiles[:, :, :32]
    out[:, 8:, :] = tiles[:, :, 32:64]


def call(kernel, outs, scratch, *args, cost=None, dtype=jnp.float32):
    places = {tuple: pltpu.SMEM, list: pl.ANY}
    estimate = {} if cost is None else dict(cost_estimate=pl.CostEstimate(flops=cost, transcendentals=0, bytes_accessed=1))
    return pl.pallas_call(
        kernel,
        out_shape=[jax.ShapeDtypeStruct(s, dtype) for s in outs],
        in_specs=[pl.BlockSpec(memory_space=places.get(type(a), pltpu.VMEM)) for a in args],
        out_specs=[pl.BlockSpec(memory_space=pltpu.VMEM) for _ in outs],
        scratch_shapes=[pltpu.VMEM(s, jnp.float32) for s in scratch],
        compiler_params=pltpu.CompilerParams(vmem_limit_bytes=VMEM_LIMIT),
        **estimate,
    )(*[a[0] if type(a) in places else a for a in args])


def move(x, step):
    return lax.ppermute(x, "dp", PAIRS[step])


def halve(own, received, after):
    half = own.shape[0] // 2

    def kernel(own, received, after, keep, give):
        give[...] = own[half:, :] + received[half:, :]
        keep[...] = own[:half, :] + received[:half, :]

    return call(kernel, [(half, B)] * 2, [], own, received, [after], cost=ADD_FLOPS)


def add(own, received, after):
    def kernel(own, received, after, out):
        out[...] = own[...] + received[...]

    return call(kernel, [own.shape], [], own, received, [after], cost=ADD_FLOPS)[0]


def join(near, far, after):
    half = near.shape[0]

    def kernel(near, far, after, out):
        out[:half, :] = near[...]
        out[half:, :] = far[...]

    return call(kernel, [(2 * half, B)], [], near, far, [after], cost=JOIN_FLOPS)[0]


WAY = ((halve, 1), (halve, 2), (add, 3), (add, 4), (add, 2), (join, 1))


def totals(first, second):
    def move_a(x, step):
        with jax.named_scope("factors"):
            return move(x, step)

    def move_b(x, step):
        with jax.named_scope("grad"):
            return move(x, step)

    def advance(own, received, after, combine, step, move):
        if combine is halve:
            own, give = halve(own, received, after)
            return own, move(give, step)
        own = combine(own, received, after)
        return own, move(own, step)

    (a, a_send), (b, b_send) = first, second
    a_in, b_in = move_a(a_send, 0), move_b(b_send, 0)
    for combine, step in WAY:
        a, a_in = advance(a, a_in, b, combine, step, move_a)
        b, b_in = advance(b, b_in, a, combine, step, move_b)
    return (a, a_in), (b, b_in)


def per_device(acts, grads_out, panel_owner):
    whole = (8 * ROWS, B)
    f_own, f_send, g_own, g_send = pl.pallas_call(
        front,
        out_shape=[jax.ShapeDtypeStruct(whole, jnp.float32)] * 4,
        in_specs=[pl.BlockSpec(memory_space=pltpu.HBM)] * 2,
        out_specs=[pl.BlockSpec(memory_space=pltpu.VMEM)] * 4,
        scratch_shapes=[pltpu.VMEM(acts.shape, acts.dtype)] * 2
        + [pltpu.VMEM((W, W), jnp.float32)] * 3
        + [pltpu.SemaphoreType.DMA((acts.shape[0] // TOKENS, 2))],
        compiler_params=pltpu.CompilerParams(vmem_limit_bytes=FRONT_LIMIT),
    )(acts, grads_out)
    (f_near, f_far), (g_near, g_far) = totals((f_own, f_send), (g_own, g_send))
    g_sum = join(g_near, g_far, f_near)
    with jax.named_scope("grad"):
        g_other = move(g_sum, 0)
    (x_own,) = call(root, [(W, W)], [whole, (W, W)], f_near, f_far, [g_near], cost=ROOT_FLOPS)
    with jax.named_scope("root"):
        x_other = move(x_own, 0)
    (begun,) = call(begin, [(W, W)], [(W // 2, W)], x_own, g_sum, cost=BEGIN_FLOPS)
    high, low = call(mix, [(W, W)] * 2, [(W // 2, W)], x_own, begun, g_other, cost=MIX_FLOPS, dtype=jnp.bfloat16)
    (tiles,) = call(finish, [(16, 8, B)], [(W, W)], (panel_owner,), high, low, x_other)
    tiles = lax.all_to_all(tiles, "mp", split_axis=0, concat_axis=0, tiled=True)
    return call(unfold, [(16, 16, 32)], [], tiles)[0]


def solution(mesh):
    return jax.shard_map(
        per_device,
        mesh=mesh,
        in_specs=(P("dp", "mp"), P("dp", "mp"), P()),
        out_specs=P(None, "dp", "mp"),
        check_vma=False,
    )
```

```python
import functools

import jax
import jax.numpy as jnp
from jax import lax
from jax.experimental import pallas as pl
from jax.experimental.pallas import tpu as pltpu
from jax.sharding import PartitionSpec as P

Z = 16
W = 512
B = 128
ROWS = 136
OFF = ((0, 1), (0, 2), (0, 3), (1, 2), (1, 3), (2, 3))
JOIN_FLOPS = 4_000_000_000
ADD_FLOPS = 0
ROOT_FLOPS = 0

BEGIN_FLOPS = 0
MIX_FLOPS = 5_000_000_000
TOKENS = 512
FRONT_LIMIT = 51 * 1024 * 1024
VMEM_LIMIT = 40 * 1024 * 1024


def partner1(v):
    return v ^ 1


def partner2(v):
    return (((v + 1) % Z) ^ 1) - 1 if ((v + 1) % Z) ^ 1 else Z - 1


def partner3(v):
    return v + 3 if v % 4 == 0 else v - 3 if v % 4 == 3 else (v + 3) % Z if v % 4 == 2 else (v - 3) % Z


def partner4(v):
    return (v + 5) % Z if v % 2 else (v - 5) % Z


QUARTER = {0: 0, 3: 0, 8: 0, 11: 0, 4: 1, 7: 1, 12: 1, 15: 1, 1: 2, 6: 2, 9: 2, 14: 2, 2: 3, 5: 3, 10: 3, 13: 3}


def holders(v, partners):
    if not partners:
        return [v]
    return holders(v, partners[:-1]) + holders(partners[-1](v), partners[:-1])


def order_code(v):
    order = [2 * QUARTER[u] + n for u in holders(v, (partner2, partner1)) for n in range(2)]
    assert sorted(order) == list(range(8))
    return sum(order.index(e) << (3 * e) for e in range(8))


def position(z, side):
    return (1 - z) % Z if side else (z + 1) % Z


def chip(v, side):
    return (1 - v) % Z if side else (v - 1) % Z


def role():
    dp = lax.axis_index("dp")
    return (dp // 2 + dp) % 2


def places(own):
    z = lax.axis_index("dp") // 2
    v = jnp.where((role() == 0) == own, (z + 1) % Z, (Z + 1 - z) % Z)
    code = jnp.int32(order_code(0))
    for u in range(1, Z):
        code = jnp.where(v == u, order_code(u), code)
    return [(code >> (3 * e)) & 7 for e in range(8)]


def device(z, side):
    return 2 * z + (z + side) % 2


def ring_pairs(partner):
    pairs = []
    for z in range(Z):
        for side in range(2):
            pairs.append((device(z, side), device(chip(partner(position(z, side)), side), side)))
    return pairs


CORE_PAIRS = [(i, i ^ 1) for i in range(2 * Z)]
PAIRS = [CORE_PAIRS] + [ring_pairs(p) for p in (partner1, partner2, partner3, partner4)]


def split(x):
    high = x.astype(jnp.bfloat16)
    low = (x - high.astype(jnp.float32)).astype(jnp.bfloat16)
    return high, low


def dot(a, b, dims=((1,), (0,))):
    return lax.dot_general(a, b, (dims, ((), ())), preferred_element_type=jnp.float32)


def product(a, b):
    (ah, al), (bh, bl) = a, b
    return dot(ah, bh) + (dot(ah, bl) + dot(al, bh))


def rows_of(index, size):
    return pl.ds(pl.multiple_of(index * ROWS, 8), size)


def put_gradient(grad, dst, half, place):
    for e in range(8):
        r, c = half * 256 + (e // 4) * B, (e % 4) * B
        dst[rows_of(place[e], B), :] = grad[r : r + B, c : c + B]
        dst[pl.ds(pl.multiple_of(place[e] * ROWS + B, 8), ROWS - B), :] = jnp.zeros((ROWS - B, B), jnp.float32)


def block_iota():
    return (lax.broadcasted_iota(jnp.int32, (B, B), n) for n in range(2))


def put_factor(src, dst, place):
    row, col = block_iota()
    for e in range(8):
        base = place[e] * ROWS
        extra = jnp.zeros((ROWS - B, B), jnp.float32)
        if e < 6:
            i, j = OFF[e]
            block = src[i * B : (i + 1) * B, j * B : (j + 1) * B]
        else:
            i = 2 * e - 12
            first = src[i * B : (i + 1) * B, i * B : (i + 1) * B]
            second = src[(i + 1) * B : (i + 2) * B, (i + 1) * B : (i + 2) * B]
            block = jnp.where(row <= col, first, second)
            extra = extra + jnp.sum(jnp.where(row == col, second, 0.0), axis=0, keepdims=True)
        dst[pl.ds(pl.multiple_of(base, 8), B), :] = block
        dst[pl.ds(pl.multiple_of(base + B, 8), ROWS - B), :] = extra


def take_factor(packed, factor, place):
    row, col = block_iota()
    for e in range(8):
        base = place[e] * ROWS
        block = packed[pl.ds(pl.multiple_of(base, 8), B), :]
        turned = block.T
        if e < 6:
            i, j = OFF[e]
            factor[i * B : (i + 1) * B, j * B : (j + 1) * B] = block
            factor[j * B : (j + 1) * B, i * B : (i + 1) * B] = turned
        else:
            i = 2 * e - 12
            diagonal = packed[pl.ds(pl.multiple_of(base + B, 8), ROWS - B), :][:1, :]
            factor[i * B : (i + 1) * B, i * B : (i + 1) * B] = jnp.where(row <= col, block, turned)
            factor[(i + 1) * B : (i + 2) * B, (i + 1) * B : (i + 2) * B] = jnp.where(
                row > col, block, jnp.where(row < col, turned, diagonal)
            )


def front(acts, grads_out, f_own, f_send, g_own, g_send, a_vmem, g_vmem, grad, left, right, sems):
    copies = []
    for i in range(acts.shape[0] // TOKENS):
        rows = pl.ds(i * TOKENS, TOKENS)
        pair = [
            pltpu.make_async_copy(src.at[rows], dst.at[rows], sems.at[i, n])
            for n, (src, dst) in enumerate(((acts, a_vmem), (grads_out, g_vmem)))
        ]
        for copy in pair:
            copy.start()
        copies.append(pair)
    place, other = places(True), places(False)
    mine = role()
    for i, pair in enumerate(copies):
        for copy in pair:
            copy.wait()
        rows = slice(i * TOKENS, (i + 1) * TOKENS)
        part = dot(a_vmem[rows, :], g_vmem[rows, :], ((0,), (0,)))
        grad[...] = part if i == 0 else grad[...] + part
    low = grad[...].astype(jnp.bfloat16)
    left[...] = dot(low, low, ((1,), (1,)))
    right[...] = dot(low, low, ((0,), (0,)))

    @pl.when(mine == 0)
    def _():
        put_factor(left, f_own, place)
        put_factor(right, f_send, other)
        put_gradient(grad, g_own, 0, place)
        put_gradient(grad, g_send, 1, other)

    @pl.when(mine == 1)
    def _():
        put_factor(right, f_own, place)
        put_factor(left, f_send, other)
        put_gradient(grad, g_own, 1, place)
        put_gradient(grad, g_send, 0, other)


def root(near, far, after, out, packed, factor):
    packed[: 4 * ROWS, :] = near[...]
    packed[4 * ROWS :, :] = far[...]
    take_factor(packed, factor, places(True))
    f = factor[...]
    norm = jnp.sqrt(jnp.sum(f * f, keepdims=True) + 1e-06)
    m1 = f / norm
    s1 = split(m1)
    m2 = product(s1, s1)
    s2 = split(m2)
    m3 = product(s2, s1)
    c = 1.0 / 4096.0
    high = (250.0 * c) * m1 - (25.0 * c) * m2 + c * m3
    low = (-5.0 / 16.0 - 3125.0 * c) * m1 + (3125.0 * c) * m2 - (1250.0 * c) * m3
    diagonal = lax.broadcasted_iota(jnp.int32, (W, W), 0) == lax.broadcasted_iota(jnp.int32, (W, W), 1)
    low = low + jnp.where(diagonal, 25.0 / 16.0, 0.0)
    x = low + product(split(m3), split(high))
    out[...] = x * lax.rsqrt(jnp.sqrt(norm))


def take_gradient(src, half, place):
    for e in range(8):
        r, c = (e // 4) * B, (e % 4) * B
        half[r : r + B, c : c + B] = src[rows_of(place[e], B), :]
    return split(half[...])


def begin(x, own, out, half):
    mine = role()
    rows = take_gradient(own, half, places(True))

    @pl.when(mine == 0)
    def _():
        out[...] = product(split(x[:, : W // 2]), rows)

    @pl.when(mine == 1)
    def _():
        out[W // 2 :, :] = product(rows, split(x[...]))
        out[: W // 2, :] = jnp.zeros((W // 2, W), jnp.float32)


def mix(x, begun, other, high, low, half):
    mine = role()
    rows = take_gradient(other, half, places(False))

    @pl.when(mine == 0)
    def _():
        high[...], low[...] = split(begun[...] + product(split(x[:, W // 2 :]), rows))

    @pl.when(mine == 1)
    def _():
        high[: W // 2, :], low[: W // 2, :] = split(product(rows, split(x[...])))
        high[W // 2 :, :], low[W // 2 :, :] = split(begun[W // 2 :, :])


def finish(owner, high, low, x, out, precond):
    mine = role()

    @pl.when(mine == 0)
    def _():
        precond[...] = product((high[...], low[...]), split(x[...]))

    @pl.when(mine == 1)
    def _():
        precond[...] = product(split(x[...]), (high[...], low[...]))

    value = precond[...]
    scale = jnp.sqrt(jnp.sum(value * value, keepdims=True) / (W * W) + 1e-06)
    panel = precond[pl.ds(pl.multiple_of(owner[lax.axis_index("dp")] * 16, 16), 16), :] / scale
    lane = lax.broadcasted_iota(jnp.int32, (8, B), 1)
    for m in range(16):
        tile = panel[:, (m // 4) * B : (m // 4 + 1) * B]
        shift = -32 * (m % 4) % B
        upper = pltpu.roll(tile[:8], shift, 1) if shift else tile[:8]
        lower = pltpu.roll(tile[8:], (shift + 32) % B, 1) if (shift + 32) % B else tile[8:]
        out[m] = jnp.where(lane < 32, upper, jnp.where(lane < 64, lower, 0.0))


def unfold(tiles, out):
    out[:, :8, :] = tiles[:, :, :32]
    out[:, 8:, :] = tiles[:, :, 32:64]


def call(kernel, outs, scratch, *args, cost=None, dtype=jnp.float32):
    places = {tuple: pltpu.SMEM, list: pl.ANY}
    estimate = {} if cost is None else dict(cost_estimate=pl.CostEstimate(flops=cost, transcendentals=0, bytes_accessed=1))
    return pl.pallas_call(
        kernel,
        out_shape=[jax.ShapeDtypeStruct(s, dtype) for s in outs],
        in_specs=[pl.BlockSpec(memory_space=places.get(type(a), pltpu.VMEM)) for a in args],
        out_specs=[pl.BlockSpec(memory_space=pltpu.VMEM) for _ in outs],
        scratch_shapes=[pltpu.VMEM(s, jnp.float32) for s in scratch],
        compiler_params=pltpu.CompilerParams(vmem_limit_bytes=VMEM_LIMIT),
        **estimate,
    )(*[a[0] if type(a) in places else a for a in args])


def move(x, step):
    return lax.ppermute(x, "dp", PAIRS[step])


def halve(own, received, after):
    half = own.shape[0] // 2

    def kernel(own, received, after, keep, give):
        give[...] = own[half:, :] + received[half:, :]
        keep[...] = own[:half, :] + received[:half, :]

    return call(kernel, [(half, B)] * 2, [], own, received, [after], cost=ADD_FLOPS)


def add(own, received, after):
    def kernel(own, received, after, out):
        out[...] = own[...] + received[...]

    return call(kernel, [own.shape], [], own, received, [after], cost=ADD_FLOPS)[0]


def join(near, far, after):
    half = near.shape[0]

    def kernel(near, far, after, out):
        out[:half, :] = near[...]
        out[half:, :] = far[...]

    return call(kernel, [(2 * half, B)], [], near, far, [after], cost=JOIN_FLOPS)[0]


WAY = ((halve, 1), (halve, 2), (add, 3), (add, 4), (add, 2), (join, 1))


def totals(first, second):
    def move_a(x, step):
        with jax.named_scope("factors"):
            return move(x, step)

    def move_b(x, step):
        with jax.named_scope("grad"):
            return move(x, step)

    def advance(own, received, after, combine, step, move):
        if combine is halve:
            own, give = halve(own, received, after)
            return own, move(give, step)
        own = combine(own, received, after)
        return own, move(own, step)

    (a, a_send), (b, b_send) = first, second
    a_in, b_in = move_a(a_send, 0), move_b(b_send, 0)
    for combine, step in WAY:
        a, a_in = advance(a, a_in, b, combine, step, move_a)
        b, b_in = advance(b, b_in, a, combine, step, move_b)
    return (a, a_in), (b, b_in)


def per_device(acts, grads_out, panel_owner):
    whole = (8 * ROWS, B)
    f_own, f_send, g_own, g_send = pl.pallas_call(
        front,
        out_shape=[jax.ShapeDtypeStruct(whole, jnp.float32)] * 4,
        in_specs=[pl.BlockSpec(memory_space=pltpu.HBM)] * 2,
        out_specs=[pl.BlockSpec(memory_space=pltpu.VMEM)] * 4,
        scratch_shapes=[pltpu.VMEM(acts.shape, acts.dtype)] * 2
        + [pltpu.VMEM((W, W), jnp.float32)] * 3
        + [pltpu.SemaphoreType.DMA((acts.shape[0] // TOKENS, 2))],
        compiler_params=pltpu.CompilerParams(vmem_limit_bytes=FRONT_LIMIT),
    )(acts, grads_out)
    (f_near, f_far), (g_near, g_far) = totals((f_own, f_send), (g_own, g_send))
    g_sum = join(g_near, g_far, f_near)
    with jax.named_scope("grad"):
        g_other = move(g_sum, 0)
    (x_own,) = call(root, [(W, W)], [whole, (W, W)], f_near, f_far, [g_near], cost=ROOT_FLOPS)
    with jax.named_scope("root"):
        x_other = move(x_own, 0)
    (begun,) = call(begin, [(W, W)], [(W // 2, W)], x_own, g_sum, cost=BEGIN_FLOPS)
    high, low = call(mix, [(W, W)] * 2, [(W // 2, W)], x_own, begun, g_other, cost=MIX_FLOPS, dtype=jnp.bfloat16)
    (tiles,) = call(finish, [(16, 8, B)], [(W, W)], (panel_owner,), high, low, x_other)
    tiles = lax.all_to_all(tiles, "mp", split_axis=0, concat_axis=0, tiled=True)
    return call(unfold, [(16, 16, 32)], [], tiles)[0]


def solution(mesh):
    return jax.shard_map(
        per_device,
        mesh=mesh,
        in_specs=(P("dp", "mp"), P("dp", "mp"), P()),
        out_specs=P(None, "dp", "mp"),
        check_vma=False,
    )
```

```python
import functools

import jax
import jax.numpy as jnp
from jax import lax
from jax.experimental import pallas as pl
from jax.experimental.pallas import tpu as pltpu
from jax.sharding import PartitionSpec as P

Z = 16
W = 512
B = 128
ROWS = 136
OFF = ((0, 1), (0, 2), (0, 3), (1, 2), (1, 3), (2, 3))
JOIN_FLOPS = 4_000_000_000
ADD_FLOPS = 0
ROOT_FLOPS = 0

BEGIN_FLOPS = 0
MIX_FLOPS = 5_000_000_000
TOKENS = 512
FRONT_LIMIT = 51 * 1024 * 1024
VMEM_LIMIT = 40 * 1024 * 1024


def partner1(v):
    return v ^ 1


def partner2(v):
    return (((v + 1) % Z) ^ 1) - 1 if ((v + 1) % Z) ^ 1 else Z - 1


def partner3(v):
    return v + 3 if v % 4 == 0 else v - 3 if v % 4 == 3 else (v + 3) % Z if v % 4 == 2 else (v - 3) % Z


def partner4(v):
    return (v + 5) % Z if v % 2 else (v - 5) % Z


QUARTER = {0: 0, 3: 0, 8: 0, 11: 0, 4: 1, 7: 1, 12: 1, 15: 1, 1: 2, 6: 2, 9: 2, 14: 2, 2: 3, 5: 3, 10: 3, 13: 3}


def holders(v, partners):
    if not partners:
        return [v]
    return holders(v, partners[:-1]) + holders(partners[-1](v), partners[:-1])


def order_code(v):
    order = [2 * QUARTER[u] + n for u in holders(v, (partner2, partner1)) for n in range(2)]
    assert sorted(order) == list(range(8))
    return sum(order.index(e) << (3 * e) for e in range(8))


def position(z, side):
    return (1 - z) % Z if side else (z + 1) % Z


def chip(v, side):
    return (1 - v) % Z if side else (v - 1) % Z


def role():
    dp = lax.axis_index("dp")
    return (dp // 2 + dp) % 2


def places(own):
    z = lax.axis_index("dp") // 2
    v = jnp.where((role() == 0) == own, (z + 1) % Z, (Z + 1 - z) % Z)
    code = jnp.int32(order_code(0))
    for u in range(1, Z):
        code = jnp.where(v == u, order_code(u), code)
    return [(code >> (3 * e)) & 7 for e in range(8)]


def device(z, side):
    return 2 * z + (z + side) % 2


def ring_pairs(partner):
    pairs = []
    for z in range(Z):
        for side in range(2):
            pairs.append((device(z, side), device(chip(partner(position(z, side)), side), side)))
    return pairs


CORE_PAIRS = [(i, i ^ 1) for i in range(2 * Z)]
PAIRS = [CORE_PAIRS] + [ring_pairs(p) for p in (partner1, partner2, partner3, partner4)]


def split(x):
    high = x.astype(jnp.bfloat16)
    low = (x - high.astype(jnp.float32)).astype(jnp.bfloat16)
    return high, low


def dot(a, b, dims=((1,), (0,))):
    return lax.dot_general(a, b, (dims, ((), ())), preferred_element_type=jnp.float32)


def product(a, b):
    (ah, al), (bh, bl) = a, b
    return dot(ah, bh) + (dot(ah, bl) + dot(al, bh))


def rows_of(index, size):
    return pl.ds(pl.multiple_of(index * ROWS, 8), size)


def put_gradient(grad, dst, half, place):
    for e in range(8):
        r, c = half * 256 + (e // 4) * B, (e % 4) * B
        dst[rows_of(place[e], B), :] = grad[r : r + B, c : c + B]
        dst[pl.ds(pl.multiple_of(place[e] * ROWS + B, 8), ROWS - B), :] = jnp.zeros((ROWS - B, B), jnp.float32)


def block_iota():
    return (lax.broadcasted_iota(jnp.int32, (B, B), n) for n in range(2))


def put_factor(src, dst, place):
    row, col = block_iota()
    for e in range(8):
        base = place[e] * ROWS
        extra = jnp.zeros((ROWS - B, B), jnp.float32)
        if e < 6:
            i, j = OFF[e]
            block = src[i * B : (i + 1) * B, j * B : (j + 1) * B]
        else:
            i = 2 * e - 12
            first = src[i * B : (i + 1) * B, i * B : (i + 1) * B]
            second = src[(i + 1) * B : (i + 2) * B, (i + 1) * B : (i + 2) * B]
            block = jnp.where(row <= col, first, second)
            extra = extra + jnp.sum(jnp.where(row == col, second, 0.0), axis=0, keepdims=True)
        dst[pl.ds(pl.multiple_of(base, 8), B), :] = block
        dst[pl.ds(pl.multiple_of(base + B, 8), ROWS - B), :] = extra


def take_factor(packed, factor, place):
    row, col = block_iota()
    for e in range(8):
        base = place[e] * ROWS
        block = packed[pl.ds(pl.multiple_of(base, 8), B), :]
        turned = block.T
        if e < 6:
            i, j = OFF[e]
            factor[i * B : (i + 1) * B, j * B : (j + 1) * B] = block
            factor[j * B : (j + 1) * B, i * B : (i + 1) * B] = turned
        else:
            i = 2 * e - 12
            diagonal = packed[pl.ds(pl.multiple_of(base + B, 8), ROWS - B), :][:1, :]
            factor[i * B : (i + 1) * B, i * B : (i + 1) * B] = jnp.where(row <= col, block, turned)
            factor[(i + 1) * B : (i + 2) * B, (i + 1) * B : (i + 2) * B] = jnp.where(
                row > col, block, jnp.where(row < col, turned, diagonal)
            )


def front(acts, grads_out, f_own, f_send, g_own, g_send, a_vmem, g_vmem, grad, left, right, sems):
    copies = []
    for i in range(acts.shape[0] // TOKENS):
        rows = pl.ds(i * TOKENS, TOKENS)
        pair = [
            pltpu.make_async_copy(src.at[rows], dst.at[rows], sems.at[i, n])
            for n, (src, dst) in enumerate(((acts, a_vmem), (grads_out, g_vmem)))
        ]
        for copy in pair:
            copy.start()
        copies.append(pair)
    place, other = places(True), places(False)
    mine = role()
    for i, pair in enumerate(copies):
        for copy in pair:
            copy.wait()
        rows = slice(i * TOKENS, (i + 1) * TOKENS)
        part = dot(a_vmem[rows, :], g_vmem[rows, :], ((0,), (0,)))
        grad[...] = part if i == 0 else grad[...] + part
    low = grad[...].astype(jnp.bfloat16)
    left[...] = dot(low, low, ((1,), (1,)))
    right[...] = dot(low, low, ((0,), (0,)))

    @pl.when(mine == 0)
    def _():
        put_factor(left, f_own, place)
        put_factor(right, f_send, other)
        put_gradient(grad, g_own, 0, place)
        put_gradient(grad, g_send, 1, other)

    @pl.when(mine == 1)
    def _():
        put_factor(right, f_own, place)
        put_factor(left, f_send, other)
        put_gradient(grad, g_own, 1, place)
        put_gradient(grad, g_send, 0, other)


def root(near, far, after, out, packed, factor):
    packed[: 4 * ROWS, :] = near[...]
    packed[4 * ROWS :, :] = far[...]
    take_factor(packed, factor, places(True))
    f = factor[...]
    norm = jnp.sqrt(jnp.sum(f * f, keepdims=True) + 1e-06)
    m1 = f / norm
    s1 = split(m1)
    m2 = product(s1, s1)
    s2 = split(m2)
    m3 = product(s2, s1)
    c = 1.0 / 4096.0
    high = (250.0 * c) * m1 - (25.0 * c) * m2 + c * m3
    low = (-5.0 / 16.0 - 3125.0 * c) * m1 + (3125.0 * c) * m2 - (1250.0 * c) * m3
    diagonal = lax.broadcasted_iota(jnp.int32, (W, W), 0) == lax.broadcasted_iota(jnp.int32, (W, W), 1)
    low = low + jnp.where(diagonal, 25.0 / 16.0, 0.0)
    cubed, rest = split(m3)
    short = high.astype(jnp.bfloat16)
    x = low + (dot(cubed, short) + dot(rest, short))
    out[...] = x * lax.rsqrt(jnp.sqrt(norm))


def take_gradient(src, half, place):
    for e in range(8):
        r, c = (e // 4) * B, (e % 4) * B
        half[r : r + B, c : c + B] = src[rows_of(place[e], B), :]
    return split(half[...])


def begin(x, own, out, half):
    mine = role()
    rows = take_gradient(own, half, places(True))

    @pl.when(mine == 0)
    def _():
        out[...] = product(split(x[:, : W // 2]), rows)

    @pl.when(mine == 1)
    def _():
        out[W // 2 :, :] = product(rows, split(x[...]))
        out[: W // 2, :] = jnp.zeros((W // 2, W), jnp.float32)


def mix(x, begun, other, high, low, half):
    mine = role()
    rows = take_gradient(other, half, places(False))

    @pl.when(mine == 0)
    def _():
        high[...], low[...] = split(begun[...] + product(split(x[:, W // 2 :]), rows))

    @pl.when(mine == 1)
    def _():
        high[: W // 2, :], low[: W // 2, :] = split(product(rows, split(x[...])))
        high[W // 2 :, :], low[W // 2 :, :] = split(begun[W // 2 :, :])


def finish(owner, high, low, x, out, precond):
    mine = role()

    @pl.when(mine == 0)
    def _():
        precond[...] = product((high[...], low[...]), split(x[...]))

    @pl.when(mine == 1)
    def _():
        precond[...] = product(split(x[...]), (high[...], low[...]))

    value = precond[...]
    scale = jnp.sqrt(jnp.sum(value * value, keepdims=True) / (W * W) + 1e-06)
    panel = precond[pl.ds(pl.multiple_of(owner[lax.axis_index("dp")] * 16, 16), 16), :] / scale
    lane = lax.broadcasted_iota(jnp.int32, (8, B), 1)
    for m in range(16):
        tile = panel[:, (m // 4) * B : (m // 4 + 1) * B]
        shift = -32 * (m % 4) % B
        upper = pltpu.roll(tile[:8], shift, 1) if shift else tile[:8]
        lower = pltpu.roll(tile[8:], (shift + 32) % B, 1) if (shift + 32) % B else tile[8:]
        out[m] = jnp.where(lane < 32, upper, jnp.where(lane < 64, lower, 0.0))


def unfold(tiles, out):
    out[:, :8, :] = tiles[:, :, :32]
    out[:, 8:, :] = tiles[:, :, 32:64]


def call(kernel, outs, scratch, *args, cost=None, dtype=jnp.float32):
    places = {tuple: pltpu.SMEM, list: pl.ANY}
    estimate = {} if cost is None else dict(cost_estimate=pl.CostEstimate(flops=cost, transcendentals=0, bytes_accessed=1))
    return pl.pallas_call(
        kernel,
        out_shape=[jax.ShapeDtypeStruct(s, dtype) for s in outs],
        in_specs=[pl.BlockSpec(memory_space=places.get(type(a), pltpu.VMEM)) for a in args],
        out_specs=[pl.BlockSpec(memory_space=pltpu.VMEM) for _ in outs],
        scratch_shapes=[pltpu.VMEM(s, jnp.float32) for s in scratch],
        compiler_params=pltpu.CompilerParams(vmem_limit_bytes=VMEM_LIMIT),
        **estimate,
    )(*[a[0] if type(a) in places else a for a in args])


def move(x, step):
    return lax.ppermute(x, "dp", PAIRS[step])


def halve(own, received, after):
    half = own.shape[0] // 2

    def kernel(own, received, after, keep, give):
        give[...] = own[half:, :] + received[half:, :]
        keep[...] = own[:half, :] + received[:half, :]

    return call(kernel, [(half, B)] * 2, [], own, received, [after], cost=ADD_FLOPS)


def add(own, received, after):
    def kernel(own, received, after, out):
        out[...] = own[...] + received[...]

    return call(kernel, [own.shape], [], own, received, [after], cost=ADD_FLOPS)[0]


def join(near, far, after):
    half = near.shape[0]

    def kernel(near, far, after, out):
        out[:half, :] = near[...]
        out[half:, :] = far[...]

    return call(kernel, [(2 * half, B)], [], near, far, [after], cost=JOIN_FLOPS)[0]


WAY = ((halve, 1), (halve, 2), (add, 3), (add, 4), (add, 2), (join, 1))


def totals(first, second):
    def move_a(x, step):
        with jax.named_scope("factors"):
            return move(x, step)

    def move_b(x, step):
        with jax.named_scope("grad"):
            return move(x, step)

    def advance(own, received, after, combine, step, move):
        if combine is halve:
            own, give = halve(own, received, after)
            return own, move(give, step)
        own = combine(own, received, after)
        return own, move(own, step)

    (a, a_send), (b, b_send) = first, second
    a_in, b_in = move_a(a_send, 0), move_b(b_send, 0)
    for combine, step in WAY:
        a, a_in = advance(a, a_in, b, combine, step, move_a)
        b, b_in = advance(b, b_in, a, combine, step, move_b)
    return (a, a_in), (b, b_in)


def per_device(acts, grads_out, panel_owner):
    whole = (8 * ROWS, B)
    f_own, f_send, g_own, g_send = pl.pallas_call(
        front,
        out_shape=[jax.ShapeDtypeStruct(whole, jnp.float32)] * 4,
        in_specs=[pl.BlockSpec(memory_space=pltpu.HBM)] * 2,
        out_specs=[pl.BlockSpec(memory_space=pltpu.VMEM)] * 4,
        scratch_shapes=[pltpu.VMEM(acts.shape, acts.dtype)] * 2
        + [pltpu.VMEM((W, W), jnp.float32)] * 3
        + [pltpu.SemaphoreType.DMA((acts.shape[0] // TOKENS, 2))],
        compiler_params=pltpu.CompilerParams(vmem_limit_bytes=FRONT_LIMIT),
    )(acts, grads_out)
    (f_near, f_far), (g_near, g_far) = totals((f_own, f_send), (g_own, g_send))
    g_sum = join(g_near, g_far, f_near)
    with jax.named_scope("grad"):
        g_other = move(g_sum, 0)
    (x_own,) = call(root, [(W, W)], [whole, (W, W)], f_near, f_far, [g_near], cost=ROOT_FLOPS)
    with jax.named_scope("root"):
        x_other = move(x_own, 0)
    (begun,) = call(begin, [(W, W)], [(W // 2, W)], x_own, g_sum, cost=BEGIN_FLOPS)
    high, low = call(mix, [(W, W)] * 2, [(W // 2, W)], x_own, begun, g_other, cost=MIX_FLOPS, dtype=jnp.bfloat16)
    (tiles,) = call(finish, [(16, 8, B)], [(W, W)], (panel_owner,), high, low, x_other)
    tiles = lax.all_to_all(tiles, "mp", split_axis=0, concat_axis=0, tiled=True)
    return call(unfold, [(16, 16, 32)], [], tiles)[0]


def solution(mesh):
    return jax.shard_map(
        per_device,
        mesh=mesh,
        in_specs=(P("dp", "mp"), P("dp", "mp"), P()),
        out_specs=P(None, "dp", "mp"),
        check_vma=False,
    )
```
